256 devices in a mesh: row: 16 (over x, y), vocab: 8 (over z), depth: 2 (over core).
Axes of the slice: x: 4, y: 4, z: 8, core: 2. Of those that a mesh axis runs over, the one named last changes fastest.
Arguments:
- hidden_state: bfloat16 [2048, 4096], P('row', 'depth'), may hold values from -13.5 to 13.5, as said below
- weight: bfloat16 [4096, 98304], P('depth', ('row', 'vocab')), may hold values from -1.5 to 1.5, as said below
- targets: int32 [2048], P('row'), may hold values from 0 to 98303
Outputs:
- loss: float32 [2048], P(('row', 'depth'))
- hidden_grad: float32 [2048, 4096], P('row', 'depth')
The draws below stay inside these ranges and needn't reach their ends.
Inputs may be any that keep to these rules, and one draw needn't show every extreme that they name: `hidden_state`: real values; each token's row has its own scale. `weight`: real values.
All inputs are finite; a program needn't handle non-finite values.
Results may differ from the reference program's by a relative error of at most 0.0012.
Values may be sent and summed in bfloat16 or wider, within the bound.
No kernel may reach another device: no remote copies, remote signals or barrier semaphores. Data moves between devices by JAX's collectives and lax.ppermute only.
A program may use at most 128 MiB of HBM per device.

```python
import jax
import jax.numpy as jnp
from jax import lax

D = 4096
TOK_DEV = 128
TOKENS = 2048
VOCAB = 98304


def aligned_picks(key):
    row_key, col_key, sign_key, gap_key = jax.random.split(key, 4)
    picked_rows = jax.random.permutation(row_key, TOKENS)[:8]
    picked_cols = jax.random.permutation(col_key, VOCAB)[:16]
    signs = jnp.where(jax.random.bernoulli(sign_key, 0.5, (8, D)), 1.0, -1.0).astype(jnp.float32)
    gaps = jax.random.uniform(gap_key, (8,), jnp.float32, 1.0, 3.0)
    pattern = jnp.where(jnp.arange(D) % 2 == 0, 1.0, -1.0).astype(jnp.float32)
    return (picked_rows, picked_cols, signs, gaps, pattern)


def draw_weight(key, part):
    picked_rows, picked_cols, signs, gaps, pattern = aligned_picks(key)
    key = jax.random.fold_in(key, 23)
    base_key, offset_key, sign_key = jax.random.split(key, 3)
    base = jnp.clip(jax.random.normal(base_key, (D, VOCAB), jnp.float32) * 0.25, -1.3, 1.3)
    offset_sign = jnp.where(jax.random.bernoulli(sign_key, 0.5, (D, 1)), 1.0, -1.0).astype(jnp.float32)
    offset = offset_sign * jax.random.uniform(offset_key, (D, 1), jnp.float32, 0.08, 0.2)
    base = base + offset
    first = (signs * 0.25).T
    second = (signs * pattern[None, :] * 0.25).T
    special = jnp.concatenate([first, second], axis=1)
    return base.at[:, picked_cols].set(special).astype(jnp.bfloat16)


def drawn_rows(key, low):
    picked_rows, picked_cols, signs, gaps, pattern = aligned_picks(key)
    strength = low + (800.0 - low) * jnp.arange(8, dtype=jnp.float32) / 7.0
    second = strength - gaps
    rows = signs * (strength[:, None] + second[:, None] * pattern[None, :]) * (4.0 / D)
    return (picked_rows, rows)


def draw_hidden_state(key, part):
    picked_rows, special = drawn_rows(key, 110.0)
    key = jax.random.fold_in(key, 11)
    first, second = jax.random.split(key)
    entries = jnp.clip(jax.random.normal(first, (TOKENS, D), jnp.float32), -5.0, 5.0)
    scales = jnp.exp(jax.random.uniform(second, (TOKENS, 1), jnp.float32, jnp.log(0.2), jnp.log(10.0)))
    base = entries * scales * 0.1875
    return base.at[picked_rows].set(special).astype(jnp.bfloat16)


def set_ends(drawn, key, least, top_value):
    spot = [jax.random.randint(jax.random.fold_in(key, axis), (), 0, length) for axis, length in enumerate(drawn.shape)]
    widest = drawn.shape.index(max(drawn.shape))
    neighbour = spot[:widest] + [(spot[widest] + 1) % drawn.shape[widest]] + spot[widest + 1:]
    return drawn.at[tuple(spot)].set(least).at[tuple(neighbour)].set(top_value)


def setup_inputs(seed: int = 0) -> dict:
    arg_keys = jax.random.split(jax.random.key(seed), 4)
    return {
        "hidden_state": draw_hidden_state(jax.random.fold_in(arg_keys[3], 71), 0),
        "weight": draw_weight(jax.random.fold_in(arg_keys[3], 71), 0),
        "targets": set_ends(jax.random.randint(arg_keys[2], (TOKENS,), 0, VOCAB), jax.random.fold_in(arg_keys[2], 1), 0, VOCAB - 1).astype(jnp.int32),
    }


def reference(hidden_state, weight, targets):
    columns = jnp.arange(VOCAB, dtype=jnp.int32)

    def block_terms(args):
        states, labels = args
        logits = jnp.dot(states, weight, preferred_element_type=jnp.float32)
        top = jnp.max(logits, axis=1, keepdims=True)
        lse = top[:, 0] + jnp.log(jnp.sum(jnp.exp(logits - top), axis=1))
        hit = columns[None, :] == labels[:, None]
        target_logit = jnp.sum(jnp.where(hit, logits, jnp.float32(0.0)), axis=1)
        probs = jnp.exp(logits - lse[:, None])
        slopes = (probs - hit.astype(jnp.float32)).astype(jnp.bfloat16)
        grad = lax.dot_general(slopes, weight, (((1,), (1,)), ((), ())), preferred_element_type=jnp.float32)
        return lse - target_logit, grad

    states = hidden_state.reshape(TOKENS // TOK_DEV, TOK_DEV, D)
    labels = targets.reshape(TOKENS // TOK_DEV, TOK_DEV)
    loss, grad = lax.map(block_terms, (states, labels))
    return loss.reshape(TOKENS), grad.reshape(TOKENS, D)
```

```python
import jax
import jax.numpy as jnp
from jax import lax
from jax.sharding import Mesh, PartitionSpec as P

F32 = jnp.float32
BF16 = jnp.bfloat16
ROW = ("x", "y")
Z = ("z4", "z2")
NX, NY, NZ4, NZ2 = 4, 4, 4, 2
PART = 32


def shift(value, axis, by):
    n = lax.axis_size(axis)
    return lax.ppermute(value, axis, [(i, (i + by) % n) for i in range(n)])


def swap(value, axis):
    return lax.ppermute(value, axis, [(0, 1), (1, 0)])


def spread(value, axis):
    n = lax.axis_size(axis)
    return lax.all_to_all(jnp.broadcast_to(value[None], (n,) + value.shape), axis, 0, 0, tiled=True)


def ring_sum(block, axis, n):
    sent = [shift(block(s), axis, s) for s in range(1, n)]
    total = block(0)
    for term in sent:
        total = total + term
    return total


def per_device(hidden_state, weight, targets):
    d = lax.axis_index("depth")
    z2 = lax.axis_index("z2")
    x = lax.axis_index("x")
    y = lax.axis_index("y")
    z = lax.axis_index("z4") * NZ2 + z2
    nz = NZ4 * NZ2
    cols = weight.shape[1]
    side = cols // 2
    half = hidden_state.shape[1]

    from_next = shift(weight[:, :side], Z, -1)
    from_prev = shift(weight[:, side:], Z, 1)

    own_part = lax.dynamic_slice(hidden_state, ((2 * d + z2) * PART, 0), (PART, half))
    other_part = lax.dynamic_slice(hidden_state, ((2 * (1 - d) + z2) * PART, 0), (PART, half))
    wide = jnp.concatenate([own_part, swap(other_part, "depth")], axis=1)
    states = lax.all_gather(wide, ROW, axis=0, tiled=True)
    labels = spread(lax.dynamic_slice(targets, ((2 * d + z2) * PART,), (PART,)), ROW).reshape(-1)
    tokens = states.shape[0]

    blocks = [weight, from_next, from_prev]
    others = [swap(b, "depth") for b in blocks]
    first = (x * NY + y) * nz
    starts = [
        (first + z) * cols,
        (first + (z + 1) % nz) * cols,
        (first + (z + nz - 1) % nz) * cols + side,
    ]
    near, far = states[:, :half], states[:, half:]
    logits, hits = [], []
    for own, other, start in zip(blocks, others, starts):
        logits.append(
            jnp.dot(near, own, preferred_element_type=F32) + jnp.dot(far, other, preferred_element_type=F32)
        )
        ids = start + jnp.arange(own.shape[1], dtype=jnp.int32)
        hits.append(ids[None, :] == labels[:, None])
    top = logits[0].max(axis=1)
    for l in logits[1:]:
        top = jnp.maximum(top, l.max(axis=1))
    total = sum(jnp.sum(jnp.exp(l - top[:, None]), axis=1) for l in logits)
    picked = sum(jnp.sum(jnp.where(h, l, 0.0), axis=1) for l, h in zip(logits, hits))
    for axis in (ROW, "z4"):
        stats = spread(jnp.stack([top, total, picked]), axis)
        tops, totals, pickeds = stats[:, 0], stats[:, 1], stats[:, 2]
        top = tops.max(axis=0)
        total = jnp.sum(totals * jnp.exp(tops - top[None]), axis=0)
        picked = jnp.sum(pickeds, axis=0)
    lse = top + jnp.log(total)

    token_loss = lax.dynamic_slice((lse - picked).reshape(NX * NY, PART), (x * NY + y, 0), (1, PART)).reshape(PART)
    loss_pair = jnp.stack([token_loss, swap(token_loss, "z2")])
    loss = jnp.where(z2 == 0, loss_pair, loss_pair[::-1]).reshape(2 * PART)

    slopes = [
        (jnp.exp(l - lse[:, None]) - h.astype(F32)).astype(BF16).reshape(NX, NY, PART, -1)
        for l, h in zip(logits, hits)
    ]

    def product(rows, weights):
        return sum(
            lax.dot_general(
                r.reshape(-1, r.shape[-1]), w, (((1,), (1,)), ((), ())), preferred_element_type=F32
            )
            for r, w in zip(rows, weights)
        )

    def by_x(s):
        at = (x + s) % NX
        return product([lax.dynamic_slice_in_dim(v, at, 1, 0) for v in slopes], blocks)

    def by_y(s):
        at = (y + s) % NY
        return product([lax.dynamic_slice_in_dim(v, at, 1, 1) for v in slopes], others)

    near_x = ring_sum(by_x, "x", NX).reshape(NY, PART, half)
    far_y = ring_sum(by_y, "y", NY).reshape(NX, PART, half)
    near_grad = ring_sum(lambda s: lax.dynamic_index_in_dim(near_x, (y + s) % NY, 0, False), "y", NY)
    far_grad = ring_sum(lambda s: lax.dynamic_index_in_dim(far_y, (x + s) % NX, 0, False), "x", NX)
    crossed = swap(far_grad, "depth")
    pair = jnp.stack([near_grad, crossed])
    pair = jnp.where(d == 0, pair, pair[::-1])
    quarter = PART // NZ4
    pair = pair.reshape(2, NZ4, quarter, half)
    z4 = lax.axis_index("z4")
    done = ring_sum(lambda s: lax.dynamic_index_in_dim(pair, (z4 + s) % NZ4, 1, False), "z4", NZ4)
    whole = lax.all_gather(done, Z, axis=0)
    grad = whole.reshape(NZ4, NZ2, 2, quarter, half).transpose(2, 1, 0, 3, 4).reshape(4 * PART, half)
    return loss, grad


def solution(mesh):
    fine = Mesh(mesh.devices.reshape(NX, NY, NZ4, NZ2, 2), ("x", "y", "z4", "z2", "depth"))
    return jax.shard_map(
        per_device,
        mesh=fine,
        in_specs=(P(ROW, "depth"), P("depth", ROW + Z), P(ROW)),
        out_specs=(P(ROW + ("depth",)), P(ROW, "depth")),
        check_vma=False,
    )
```

```python
import functools

import jax
import jax.numpy as jnp
from jax import lax
from jax.experimental import pallas as pl
from jax.experimental.pallas import tpu as pltpu
from jax.sharding import Mesh, PartitionSpec as P

F32 = jnp.float32
BF16 = jnp.bfloat16
I32 = jnp.int32
ROW = ("x", "y")
Z = ("z4", "z2")
NX, NY, NZ4, NZ2 = 4, 4, 4, 2
NROW = NX * NY
PART = 32
QUARTER = PART // NZ4
LANES = 128
CHUNK = 32
MIB = 1024 * 1024
ANY = pl.BlockSpec(memory_space=pl.ANY)
SMEM = pl.BlockSpec(memory_space=pltpu.SMEM)
VMEM = pl.BlockSpec(memory_space=pltpu.VMEM)


def shift(value, axis, by):
    n = lax.axis_size(axis)
    return lax.ppermute(value, axis, [(i, (i + by) % n) for i in range(n)])


def swap(value, axis):
    return lax.ppermute(value, axis, [(0, 1), (1, 0)])


def spread(value, axis):
    n = lax.axis_size(axis)
    return lax.all_to_all(jnp.broadcast_to(value[None], (n,) + value.shape), axis, 0, 0, tiled=True)


def ring_copies(value, axis, n):
    return [value] + [shift(value, axis, s) for s in range(1, n)]


def column(row_ref, tokens):
    return jnp.transpose(jnp.broadcast_to(row_ref[0:1, :], (LANES, tokens)))


def logits_kernel(at_ref, labels_ref, ids_ref, *refs):
    near, far, weights = refs[:NY], refs[NY : NY + NX], refs[NY + NX : NY + NX + 6]
    logits_ref, stats_ref, xn, xf, wn, wf, lab, col, sems = refs[NY + NX + 6 :]
    x, y = at_ref[0], at_ref[1]
    tokens, cols = logits_ref.shape
    own = weights[0].shape[1]
    side = weights[1].shape[1]
    first, rest = [], []

    def copy(group, src, dst):
        c = pltpu.make_async_copy(src, dst, sems.at[len(first) + len(rest)])
        c.start()
        group.append(c)

    def place(i, j):
        return pl.ds(pl.multiple_of((((x - i) & 3) * NY + ((y - j) & 3)) * PART, PART), PART)

    for j in range(NY):
        for i in range(NX):
            copy(first, near[j].at[i], xn.at[place(i, j)])
    copy(first, weights[0], wn.at[:, pl.ds(0, own)])
    for i in range(NX):
        for j in range(NY):
            copy(first, far[i].at[j], xf.at[place(i, j)])
    copy(first, weights[3], wf.at[:, pl.ds(0, own)])
    copy(rest, weights[1], wn.at[:, pl.ds(own, side)])
    copy(rest, weights[2], wn.at[:, pl.ds(own + side, side)])
    copy(rest, weights[4], wf.at[:, pl.ds(own, side)])
    copy(rest, weights[5], wf.at[:, pl.ds(own + side, side)])
    lab[...] = column(labels_ref, tokens)

    def tile(t, _):
        c = pl.ds(pl.multiple_of(t * 256, 256), 256)
        logits_ref[:, c] = jnp.dot(xn[...], wn[:, c], preferred_element_type=F32) + jnp.dot(
            xf[...], wf[:, c], preferred_element_type=F32
        )
        return 0

    for c in first:
        c.wait()
    lax.fori_loop(0, own // 256, tile, 0)
    for c in rest:
        c.wait()
    lax.fori_loop(own // 256, cols // 256, tile, 0)

    def chunk(k, _):
        r = pl.ds(pl.multiple_of(k * CHUNK, CHUNK), CHUNK)
        v = logits_ref[r, :]
        top = jnp.max(v, axis=1, keepdims=True)
        total = jnp.sum(jnp.exp(v - top), axis=1, keepdims=True)
        hit = ids_ref[0:1, :] == lab[r, 0:1]
        picked = jnp.sum(jnp.where(hit, v, 0.0), axis=1, keepdims=True)
        lane = lax.broadcasted_iota(I32, (CHUNK, LANES), 1)
        col[r, :] = jnp.where(lane == 0, top, jnp.where(lane == 1, total, picked))
        return 0

    lax.fori_loop(0, tokens // CHUNK, chunk, 0)
    stats_ref[...] = jnp.transpose(col[...])[0:8, :]


def logits_call(at, labels, ids, near, far, weights):
    half = near[0].shape[-1]
    tokens = labels.shape[1]
    cols = ids.shape[1]
    copies = 2 * NROW + 6
    return pl.pallas_call(
        logits_kernel,
        out_shape=(
            jax.ShapeDtypeStruct((tokens, cols), F32),
            jax.ShapeDtypeStruct((8, tokens), F32),
        ),
        in_specs=[SMEM, VMEM, VMEM] + [ANY] * (NX + NY + 6),
        out_specs=(VMEM, VMEM),
        scratch_shapes=[
            pltpu.VMEM((tokens, half), BF16),
            pltpu.VMEM((tokens, half), BF16),
            pltpu.VMEM((half, cols), BF16),
            pltpu.VMEM((half, cols), BF16),
            pltpu.VMEM((tokens, LANES), I32),
            pltpu.VMEM((tokens, LANES), F32),
            pltpu.SemaphoreType.DMA((copies,)),
        ],
        compiler_params=pltpu.CompilerParams(vmem_limit_bytes=40 * MIB),
        cost_estimate=pl.CostEstimate(
            flops=4 * tokens * half * cols, bytes_accessed=20 * MIB, transcendentals=tokens * cols
        ),
        name="logits",
    )(at, labels, ids, *near, *far, *weights)


def contract(slopes, w0, w1, w2):
    own, side = w0.shape[1], w1.shape[1]

    def nt(a, b):
        return lax.dot_general(a, b, (((1,), (1,)), ((), ())), preferred_element_type=F32)

    return (
        nt(slopes[:, 0:own], w0[...])
        + nt(slopes[:, own : own + side], w1[...])
        + nt(slopes[:, own + side :], w2[...])
    )


def near_kernel(at_ref, labels_ref, ids_ref, lse_ref, logits_ref, w0, w1, w2, *refs):
    outs, (slopes_ref, lab, lse, acc) = refs[:NX], refs[NX:]
    x = at_ref[0]
    tokens = logits_ref.shape[0]
    span = tokens // NX

    @pl.when(pl.program_id(0) == 0)
    def _():
        lab[...] = column(labels_ref, tokens)
        lse[...] = column(lse_ref, tokens)

        def chunk(k, _):
            r = pl.ds(pl.multiple_of(k * CHUNK, CHUNK), CHUNK)
            hit = ids_ref[0:1, :] == lab[r, 0:1]
            p = jnp.exp(logits_ref[r, :] - lse[r, 0:1])
            slopes_ref[r, :] = (p - jnp.where(hit, 1.0, 0.0)).astype(BF16)
            return 0

        lax.fori_loop(0, tokens // CHUNK, chunk, 0)

    acc[...] = contract(slopes_ref, w0, w1, w2)
    for s in range(NX):
        outs[s][...] = acc[pl.ds(pl.multiple_of(((x + s) & 3) * span, span), span), :]


def far_kernel(at_ref, slopes_ref, w0, w1, w2, *refs):
    outs, (acc,) = refs[:NY], refs[NY:]
    y = at_ref[1]
    acc[...] = contract(slopes_ref, w0, w1, w2)
    for s in range(NY):
        for a in range(NX):
            rows = pl.ds(pl.multiple_of((a * NY + ((y + s) & 3)) * PART, PART), PART)
            outs[s][pl.ds(a * PART, PART), :] = acc[rows, :]


TILE = 512


def product_call(kernel, heads, head_specs, weights, tokens, extra_out, extra_scratch, name):
    half = weights[0].shape[0]
    n = NX
    outs = [jax.ShapeDtypeStruct((tokens // n, half), F32)] * n
    specs = [pl.BlockSpec((tokens // n, TILE), lambda g: (0, g))] * n
    for e in extra_out:
        outs.append(e)
        specs.append(pl.BlockSpec(e.shape, lambda g: (0, 0)))
    cols = sum(w.shape[1] for w in weights)
    return pl.pallas_call(
        kernel,
        grid=(half // TILE,),
        out_shape=tuple(outs),
        in_specs=head_specs + [pl.BlockSpec((TILE, w.shape[1]), lambda g: (g, 0)) for w in weights],
        out_specs=tuple(specs),
        scratch_shapes=extra_scratch + [pltpu.VMEM((tokens, TILE), F32)],
        compiler_params=pltpu.CompilerParams(vmem_limit_bytes=40 * MIB),
        cost_estimate=pl.CostEstimate(
            flops=2 * tokens * half * cols, bytes_accessed=12 * MIB, transcendentals=0
        ),
        name=name,
    )(*heads, *weights)


def whole_block(shape):
    return pl.BlockSpec(shape, lambda g: (0,) * len(shape))


def assemble_kernel(at_ref, own0, own1, other0, other1, out, sems):
    z4, z2 = at_ref[2], at_ref[3]
    up = (z4 + z2) & 3
    down = (z4 + z2 + 3) & 3
    copies = []
    for core, (src, parity, base) in enumerate(
        ((own0, z2, z4), (own1, z2, z4), (other0, 1 - z2, up), (other1, 1 - z2, down))
    ):
        for k in range(NZ4):
            copies.append(
                pltpu.make_async_copy(
                    src.at[k], out.at[core % 2, parity, (base - k) & 3], sems.at[core * NZ4 + k]
                )
            )
    for c in copies:
        c.start()
    for c in copies:
        c.wait()


def assemble_call(at, own0, own1, other0, other1):
    half = own0.shape[-1]
    return pl.pallas_call(
        assemble_kernel,
        out_shape=jax.ShapeDtypeStruct((2, NZ2, NZ4, QUARTER, half), F32),
        in_specs=[SMEM] + [ANY] * 4,
        out_specs=ANY,
        scratch_shapes=[pltpu.SemaphoreType.DMA((4 * NZ4,))],
        compiler_params=pltpu.CompilerParams(vmem_limit_bytes=40 * MIB),
        name="assemble",
    )(at, own0, own1, other0, other1)


def per_device(hidden_state, weight, targets):
    d = lax.axis_index("depth")
    z2 = lax.axis_index("z2")
    z4 = lax.axis_index("z4")
    x = lax.axis_index("x")
    y = lax.axis_index("y")
    z = z4 * NZ2 + z2
    nz = NZ4 * NZ2
    cols = weight.shape[1]
    side = cols // 2
    half = hidden_state.shape[1]
    tokens = NROW * PART
    at = jnp.stack([x, y, z4, z2]).astype(I32)

    near = lax.dynamic_slice(hidden_state, ((2 * d + z2) * PART, 0), (PART, half))
    far = swap(lax.dynamic_slice(hidden_state, ((2 * (1 - d) + z2) * PART, 0), (PART, half)), "depth")
    near_blocks = ring_copies(jnp.stack(ring_copies(near, "x", NX)), "y", NY)
    far_blocks = ring_copies(jnp.stack(ring_copies(far, "y", NY)), "x", NX)

    from_next = shift(weight[:, :side], Z, -1)
    from_prev = shift(weight[:, side:], Z, 1)
    labels = spread(lax.dynamic_slice(targets, ((2 * d + z2) * PART,), (PART,)), ROW).reshape(-1)
    labels = jnp.broadcast_to(labels[None], (8, tokens))

    blocks = [weight, from_next, from_prev]
    others = [swap(b, "depth") for b in blocks]
    first = (x * NY + y) * nz
    starts = [
        (first + z) * cols,
        (first + (z + 1) % nz) * cols,
        (first + (z + nz - 1) % nz) * cols + side,
    ]
    ids = jnp.concatenate([s + jnp.arange(b.shape[1], dtype=I32) for s, b in zip(starts, blocks)])
    ids = jnp.broadcast_to(ids[None], (8, ids.shape[0]))

    logits, stats = logits_call(at, labels, ids, near_blocks, far_blocks, blocks + others)
    top, total, picked = stats[0], stats[1], stats[2]
    for axis in (ROW, "z4"):
        stats = spread(jnp.stack([top, total, picked]), axis)
        tops, totals, pickeds = stats[:, 0], stats[:, 1], stats[:, 2]
        top = tops.max(axis=0)
        total = jnp.sum(totals * jnp.exp(tops - top[None]), axis=0)
        picked = jnp.sum(pickeds, axis=0)
    lse = top + jnp.log(total)

    token_loss = lax.dynamic_slice((lse - picked).reshape(NROW, PART), (x * NY + y, 0), (1, PART)).reshape(PART)
    loss_pair = jnp.stack([token_loss, swap(token_loss, "z2")])
    loss = jnp.where(z2 == 0, loss_pair, loss_pair[::-1]).reshape(2 * PART)

    row_spec = whole_block((8, tokens))
    *near_out, slopes = product_call(
        near_kernel,
        [at, labels, ids, jnp.broadcast_to(lse[None], (8, tokens)), logits],
        [SMEM, row_spec, whole_block(ids.shape), row_spec, whole_block(logits.shape)],
        blocks,
        tokens,
        [jax.ShapeDtypeStruct(logits.shape, BF16)],
        [pltpu.VMEM((tokens, LANES), I32), pltpu.VMEM((tokens, LANES), F32)],
        "near_grad",
    )
    far_out = product_call(
        far_kernel, [at, slopes], [SMEM, whole_block(slopes.shape)], others, tokens, [], [], "far_grad"
    )

    def ring_sum(parts, axis):
        terms = [parts[0]] + [shift(p, axis, s) for s, p in enumerate(parts) if s]
        return terms[0] + terms[1] + terms[2] + terms[3]

    near_x = ring_sum(near_out, "x").reshape(NY, PART, half)
    far_y = ring_sum(far_out, "y").reshape(NX, PART, half)
    near_grad = ring_sum([lax.dynamic_index_in_dim(near_x, (y + s) % NY, 0, False) for s in range(NY)], "y")
    far_grad = ring_sum([lax.dynamic_index_in_dim(far_y, (x + s) % NX, 0, False) for s in range(NX)], "x")
    crossed = swap(far_grad, "depth")
    pair = jnp.stack([near_grad, crossed])
    pair = jnp.where(d == 0, pair, pair[::-1]).reshape(2, NZ4, QUARTER, half)
    done = ring_sum([lax.dynamic_index_in_dim(pair, (z4 + s) % NZ4, 1, False) for s in range(NZ4)], "z4")
    copies = ring_copies(done, "z4", NZ4)
    own0 = jnp.stack([c[0] for c in copies])
    own1 = jnp.stack([c[1] for c in copies])
    other0 = shift(own0, Z, -1)
    other1 = shift(own1, Z, 1)
    grad = assemble_call(at, own0, own1, other0, other1).reshape(4 * PART, half)
    return loss, grad


def solution(mesh):
    fine = Mesh(mesh.devices.reshape(NX, NY, NZ4, NZ2, 2), ("x", "y", "z4", "z2", "depth"))
    return jax.shard_map(
        per_device,
        mesh=fine,
        in_specs=(P(ROW, "depth"), P("depth", ROW + Z), P(ROW)),
        out_specs=(P(ROW + ("depth",)), P(ROW, "depth")),
        check_vma=False,
    )
```

```python
import functools

import jax
import jax.numpy as jnp
from jax import lax
from jax.experimental import pallas as pl
from jax.experimental.pallas import tpu as pltpu
from jax.sharding import Mesh, PartitionSpec as P

F32 = jnp.float32
BF16 = jnp.bfloat16
I32 = jnp.int32
ROW = ("x", "y")
Z = ("z4", "z2")
NX, NY, NZ4, NZ2 = 4, 4, 4, 2
NROW = NX * NY
PART = 32
QUARTER = PART // NZ4
LANES = 128
CHUNK = 32
FLIGHT = 3
TILE = 512
MIB = 1024 * 1024
ANY = pl.BlockSpec(memory_space=pl.ANY)
SMEM = pl.BlockSpec(memory_space=pltpu.SMEM)
VMEM = pl.BlockSpec(memory_space=pltpu.VMEM)


def shift(value, axis, by):
    n = lax.axis_size(axis)
    return lax.ppermute(value, axis, [(i, (i + by) % n) for i in range(n)])


def swap(value, axis):
    return lax.ppermute(value, axis, [(0, 1), (1, 0)])


def cross_shift(value, axis, by):
    n = lax.axis_size(axis)
    pairs = [(2 * i + c, 2 * ((i + by) % n) + 1 - c) for i in range(n) for c in range(2)]
    return lax.ppermute(value, (axis, "depth"), pairs)


def after(value, earlier):
    return lax.optimization_barrier((value, earlier))[0]


def spread(value, axis):
    n = lax.axis_size(axis)
    return lax.all_to_all(jnp.broadcast_to(value[None], (n,) + value.shape), axis, 0, 0, tiled=True)


def ring_copies(value, axis, n):
    return [value] + [shift(value, axis, s) for s in range(1, n)]


def column(row_ref, tokens):
    return jnp.transpose(jnp.broadcast_to(row_ref[0:1, :], (LANES, tokens)))


def logits_kernel(at_ref, ids_ref, *refs):
    near, far, weights = refs[:NY], refs[NY : NY + NX], refs[NY + NX : NY + NX + 10]
    logits_ref, stats_ref, lab, xn, xf, wn, wf, digits, col, sems = refs[NY + NX + 10 :]
    x, y = at_ref[0], at_ref[1]
    tokens, cols = logits_ref.shape
    own = weights[0].shape[1]
    side = weights[1].shape[1]
    half = weights[0].shape[0]
    first, rest = [], []

    def copy(group, src, dst):
        c = pltpu.make_async_copy(src, dst, sems.at[len(first) + len(rest)])
        c.start()
        group.append(c)

    def place(i, j):
        return pl.ds(pl.multiple_of((((x - i) & 3) * NY + ((y - j) & 3)) * PART, PART), PART)

    for j in range(NY):
        for i in range(NX):
            copy(first, near[j].at[i, :, pl.ds(0, half)], xn.at[place(i, j)])
            copy(first, near[j].at[i, :, pl.ds(half, LANES)], digits.at[place(i, j)])
    copy(first, weights[0], wn.at[:, pl.ds(0, own)])
    for i in range(NX):
        for j in range(NY):
            copy(first, far[i].at[j], xf.at[place(i, j)])
    copy(first, weights[5], wf.at[:, pl.ds(0, own)])
    for w, full in enumerate((wn, wf)):
        for k in range(4):
            piece = weights[5 * w + 1 + k]
            rows = pl.ds(0, TILE) if k % 2 == 0 else pl.ds(TILE, half - TILE)
            copy(rest, piece, full.at[rows, pl.ds(own + side * (k // 2), side)])

    def tile(t, _):
        c = pl.ds(pl.multiple_of(t * 256, 256), 256)
        logits_ref[:, c] = jnp.dot(xn[...], wn[:, c], preferred_element_type=F32) + jnp.dot(
            xf[...], wf[:, c], preferred_element_type=F32
        )
        return 0

    for c in first:
        c.wait()
    lax.fori_loop(0, own // 256, tile, 0)
    v = digits[...].astype(F32)
    code = v[:, 0:1] + 256.0 * v[:, 1:2] + 65536.0 * v[:, 2:3]
    lab[...] = jnp.broadcast_to(code, (tokens, LANES)).astype(I32)
    for c in rest:
        c.wait()
    lax.fori_loop(own // 256, cols // 256, tile, 0)

    def chunk(k, _):
        r = pl.ds(pl.multiple_of(k * CHUNK, CHUNK), CHUNK)
        v = logits_ref[r, :]
        top = jnp.max(v, axis=1, keepdims=True)
        total = jnp.sum(jnp.exp(v - top), axis=1, keepdims=True)
        hit = ids_ref[0:1, :] == lab[r, 0:1]
        picked = jnp.sum(jnp.where(hit, v, 0.0), axis=1, keepdims=True)
        lane = lax.broadcasted_iota(I32, (CHUNK, LANES), 1)
        col[r, :] = jnp.where(lane == 0, top, jnp.where(lane == 1, total, picked))
        return 0

    lax.fori_loop(0, tokens // CHUNK, chunk, 0)
    stats_ref[...] = jnp.transpose(col[...])[0:8, :]


def logits_call(at, ids, near, far, weights):
    half = far[0].shape[-1]
    tokens = NROW * PART
    cols = ids.shape[1]
    copies = 3 * NROW + 10
    return pl.pallas_call(
        logits_kernel,
        out_shape=(
            jax.ShapeDtypeStruct((tokens, cols), F32),
            jax.ShapeDtypeStruct((8, tokens), F32),
            jax.ShapeDtypeStruct((tokens, LANES), I32),
        ),
        in_specs=[SMEM, VMEM] + [ANY] * (NX + NY + 10),
        out_specs=(VMEM, VMEM, VMEM),
        scratch_shapes=[
            pltpu.VMEM((tokens, half), BF16),
            pltpu.VMEM((tokens, half), BF16),
            pltpu.VMEM((half, cols), BF16),
            pltpu.VMEM((half, cols), BF16),
            pltpu.VMEM((tokens, LANES), BF16),
            pltpu.VMEM((tokens, LANES), F32),
            pltpu.SemaphoreType.DMA((copies,)),
        ],
        compiler_params=pltpu.CompilerParams(vmem_limit_bytes=40 * MIB),
        cost_estimate=pl.CostEstimate(
            flops=4 * tokens * half * cols, bytes_accessed=20 * MIB, transcendentals=tokens * cols
        ),
        name="logits",
    )(at, ids, *near, *far, *weights)


def contract(acc, slopes, w0, next_a, next_b, prev_a, prev_b):
    own, side = w0.shape[1], next_a.shape[1]

    def nt(a, b):
        return lax.dot_general(a, b, (((1,), (1,)), ((), ())), preferred_element_type=F32)

    def tile(w1, w2):
        acc[...] = (
            nt(slopes[:, 0:own], w0[...])
            + nt(slopes[:, own : own + side], w1[...])
            + nt(slopes[:, own + side :], w2[...])
        )

    pl.when(pl.program_id(0) == 0)(lambda: tile(next_a, prev_a))
    pl.when(pl.program_id(0) > 0)(lambda: tile(next_b, prev_b))


def near_kernel(at_ref, lab, ids_ref, lse_ref, logits_ref, *refs):
    weights, outs, (slopes_ref, lse, acc) = refs[:5], refs[5 : 5 + NX], refs[5 + NX :]
    x = at_ref[0]
    tokens = logits_ref.shape[0]
    span = tokens // NX

    @pl.when(pl.program_id(0) == 0)
    def _():
        lse[...] = column(lse_ref, tokens)

        def chunk(k, _):
            r = pl.ds(pl.multiple_of(k * CHUNK, CHUNK), CHUNK)
            hit = ids_ref[0:1, :] == lab[r, 0:1]
            p = jnp.exp(logits_ref[r, :] - lse[r, 0:1])
            slopes_ref[r, :] = (p - jnp.where(hit, 1.0, 0.0)).astype(BF16)
            return 0

        lax.fori_loop(0, tokens // CHUNK, chunk, 0)

    contract(acc, slopes_ref, *weights)
    for s in range(NX):
        outs[s][...] = acc[pl.ds(pl.multiple_of(((x + s) & 3) * span, span), span), :]


def far_kernel(at_ref, slopes_ref, *refs):
    weights, outs, (acc,) = refs[:5], refs[5 : 5 + NY], refs[5 + NY :]
    y = at_ref[1]
    contract(acc, slopes_ref, *weights)
    for s in range(NY):
        for a in range(NX):
            rows = pl.ds(pl.multiple_of((a * NY + ((y + s) & 3)) * PART, PART), PART)
            outs[s][pl.ds(a * PART, PART), :] = acc[rows, :]


def product_call(kernel, heads, head_specs, weights, tokens, extra_out, extra_scratch, name):
    half = weights[0].shape[0]
    n = NX
    outs = [jax.ShapeDtypeStruct((tokens // n, half), F32)] * n
    specs = [pl.BlockSpec((tokens // n, TILE), lambda g: (0, g))] * n
    for e in extra_out:
        outs.append(e)
        specs.append(pl.BlockSpec(e.shape, lambda g: (0, 0)))
    cols = weights[0].shape[1] * 2
    here, first, later = (lambda g: (g, 0)), (lambda g: (0, 0)), (lambda g: (jnp.maximum(g - 1, 0), 0))
    maps = [here, first, later, first, later]
    return pl.pallas_call(
        kernel,
        grid=(half // TILE,),
        out_shape=tuple(outs),
        in_specs=head_specs + [pl.BlockSpec((TILE, w.shape[1]), m) for w, m in zip(weights, maps)],
        out_specs=tuple(specs),
        scratch_shapes=extra_scratch + [pltpu.VMEM((tokens, TILE), F32)],
        compiler_params=pltpu.CompilerParams(vmem_limit_bytes=40 * MIB),
        cost_estimate=pl.CostEstimate(
            flops=2 * tokens * half * cols, bytes_accessed=12 * MIB, transcendentals=0
        ),
        name=name,
    )(*heads, *weights)


def whole_block(shape):
    return pl.BlockSpec(shape, lambda g: (0,) * len(shape))


def assemble_kernel(at_ref, own0, own1, other0, other1, out, sems):
    z4, z2 = at_ref[2], at_ref[3]
    up = (z4 + z2) & 3
    down = (z4 + z2 + 3) & 3
    copies = []
    for core, (src, parity, base) in enumerate(
        ((own0, z2, z4), (own1, z2, z4), (other0, 1 - z2, up), (other1, 1 - z2, down))
    ):
        for k in range(NZ4):
            copies.append(
                pltpu.make_async_copy(
                    src.at[k], out.at[core % 2, parity, (base - k) & 3], sems.at[core * NZ4 + k]
                )
            )
    for c in copies:
        c.start()
    for c in copies:
        c.wait()


def assemble_call(at, own0, own1, other0, other1):
    half = own0.shape[-1]
    return pl.pallas_call(
        assemble_kernel,
        out_shape=jax.ShapeDtypeStruct((2, NZ2, NZ4, QUARTER, half), F32),
        in_specs=[SMEM] + [ANY] * 4,
        out_specs=ANY,
        scratch_shapes=[pltpu.SemaphoreType.DMA((4 * NZ4,))],
        compiler_params=pltpu.CompilerParams(vmem_limit_bytes=40 * MIB),
        name="assemble",
    )(at, own0, own1, other0, other1)


def per_device(hidden_state, weight, targets):
    d = lax.axis_index("depth")
    z2 = lax.axis_index("z2")
    z4 = lax.axis_index("z4")
    x = lax.axis_index("x")
    y = lax.axis_index("y")
    z = z4 * NZ2 + z2
    nz = NZ4 * NZ2
    cols = weight.shape[1]
    side = cols // 2
    half = hidden_state.shape[1]
    tokens = NROW * PART
    at = jnp.stack([x, y, z4, z2]).astype(I32)

    near = lax.dynamic_slice(hidden_state, ((2 * d + z2) * PART, 0), (PART, half))
    crossing = lax.dynamic_slice(hidden_state, ((2 * (1 - d) + z2) * PART, 0), (PART, half))
    label = lax.dynamic_slice(targets, ((2 * d + z2) * PART,), (PART,))
    digits = jnp.stack([label % 256, (label // 256) % 256, label // 65536], axis=1).astype(BF16)
    near = jnp.concatenate([near, jnp.pad(digits, ((0, 0), (0, LANES - 3)))], axis=1)

    left, right = weight[:, :side], weight[:, side:]
    cut = TILE
    small = []

    def queued(value, axis, by, cross=False):
        if len(small) >= FLIGHT:
            value = after(value, small[-FLIGHT])
        small.append(cross_shift(value, axis, by) if cross else shift(value, axis, by))
        return small[-1]

    next_a, prev_a = shift(left[:cut], Z, -1), shift(right[:cut], Z, 1)
    far_parts = {0: queued(crossing, "y", 0, True)}
    near_parts = {0: near}
    for s in (1, 3, 2):
        near_parts[s] = queued(near, "x", s)
        far_parts[s] = queued(crossing, "y", s, True)
    near_line = jnp.stack([near_parts[s] for s in range(NX)])
    far_line = jnp.stack([far_parts[s] for s in range(NY)])

    near_line, far_line, left_b, right_b = lax.optimization_barrier(
        (near_line, far_line, left[cut:], right[cut:], next_a, prev_a)
    )[:4]
    next_b, prev_b = shift(left_b, Z, -1), shift(right_b, Z, 1)
    near_blocks, far_blocks = {0: near_line}, {0: far_line}
    for s in (1, 3):
        near_blocks[s] = shift(near_line, "y", s)
        far_blocks[s] = shift(far_line, "x", s)

    near_last, far_last, own, next_a, prev_a, next_b, prev_b = lax.optimization_barrier(
        (near_line, far_line, weight, next_a, prev_a, next_b, prev_b)
        + (near_blocks[1], far_blocks[1], near_blocks[3], far_blocks[3])
    )[:7]
    near_blocks[2] = shift(near_last, "y", 2)
    far_blocks[2] = shift(far_last, "x", 2)
    near_blocks = [near_blocks[s] for s in range(NY)]
    far_blocks = [far_blocks[s] for s in range(NX)]
    pieces = [weight, next_a, next_b, prev_a, prev_b]
    others = [swap(b, "depth") for b in (own, next_a, next_b, prev_a, prev_b)]
    first = (x * NY + y) * nz
    starts = [
        (first + z) * cols,
        (first + (z + 1) % nz) * cols,
        (first + (z + nz - 1) % nz) * cols + side,
    ]
    ids = jnp.concatenate([s + jnp.arange(n, dtype=I32) for s, n in zip(starts, (cols, side, side))])
    ids = jnp.broadcast_to(ids[None], (8, ids.shape[0]))

    logits, stats, labels = logits_call(at, ids, near_blocks, far_blocks, pieces + others)
    top, total, picked = stats[0], stats[1], stats[2]
    for axis in (ROW, "z4"):
        stats = spread(jnp.stack([top, total, picked]), axis)
        tops, totals, pickeds = stats[:, 0], stats[:, 1], stats[:, 2]
        top = tops.max(axis=0)
        total = jnp.sum(totals * jnp.exp(tops - top[None]), axis=0)
        picked = jnp.sum(pickeds, axis=0)
    lse = top + jnp.log(total)

    token_loss = lax.dynamic_slice((lse - picked).reshape(NROW, PART), (x * NY + y, 0), (1, PART)).reshape(PART)
    loss_pair = jnp.stack([token_loss, swap(token_loss, "z2")])
    loss = jnp.where(z2 == 0, loss_pair, loss_pair[::-1]).reshape(2 * PART)

    row_spec = whole_block((8, tokens))
    *near_out, slopes = product_call(
        near_kernel,
        [at, labels, ids, jnp.broadcast_to(lse[None], (8, tokens)), logits],
        [SMEM, whole_block(labels.shape), whole_block(ids.shape), row_spec, whole_block(logits.shape)],
        pieces,
        tokens,
        [jax.ShapeDtypeStruct(logits.shape, BF16)],
        [pltpu.VMEM((tokens, LANES), F32)],
        "near_grad",
    )
    far_out = product_call(
        far_kernel, [at, slopes], [SMEM, whole_block(slopes.shape)], others, tokens, [], [], "far_grad"
    )

    def ring_sum(parts, axis):
        terms = [parts[0]] + [shift(p, axis, s) for s, p in enumerate(parts) if s]
        return terms[0] + terms[1] + terms[2] + terms[3]

    near_x = ring_sum(near_out, "x").reshape(NY, PART, half)
    far_y = ring_sum(far_out, "y").reshape(NX, PART, half)
    near_grad = ring_sum([lax.dynamic_index_in_dim(near_x, (y + s) % NY, 0, False) for s in range(NY)], "y")
    far_grad = ring_sum([lax.dynamic_index_in_dim(far_y, (x + s) % NX, 0, False) for s in range(NX)], "x")
    crossed = swap(far_grad, "depth")
    pair = jnp.stack([near_grad, crossed])
    pair = jnp.where(d == 0, pair, pair[::-1]).reshape(2, NZ4, QUARTER, half)
    done = ring_sum([lax.dynamic_index_in_dim(pair, (z4 + s) % NZ4, 1, False) for s in range(NZ4)], "z4")
    copies = ring_copies(done, "z4", NZ4)
    own0 = jnp.stack([c[0] for c in copies])
    own1 = jnp.stack([c[1] for c in copies])
    other0 = shift(own0, Z, -1)
    other1 = shift(own1, Z, 1)
    grad = assemble_call(at, own0, own1, other0, other1).reshape(4 * PART, half)
    return loss, grad


def solution(mesh):
    fine = Mesh(mesh.devices.reshape(NX, NY, NZ4, NZ2, 2), ("x", "y", "z4", "z2", "depth"))
    return jax.shard_map(
        per_device,
        mesh=fine,
        in_specs=(P(ROW, "depth"), P("depth", ROW + Z), P(ROW)),
        out_specs=(P(ROW + ("depth",)), P(ROW, "depth")),
        check_vma=False,
    )
```

```python
import functools

import jax
import jax.numpy as jnp
from jax import lax
from jax.experimental import pallas as pl
from jax.experimental.pallas import tpu as pltpu
from jax.sharding import Mesh, PartitionSpec as P

F32 = jnp.float32
BF16 = jnp.bfloat16
I32 = jnp.int32
ROW = ("x", "y")
Z = ("z4", "z2")
NX, NY, NZ4, NZ2 = 4, 4, 4, 2
NROW = NX * NY
PART = 32
QUARTER = PART // NZ4
LANES = 128
CHUNK = 32
WIDE = 256
TILE = 512
MIB = 1024 * 1024
ANY = pl.BlockSpec(memory_space=pl.ANY)
SMEM = pl.BlockSpec(memory_space=pltpu.SMEM)
VMEM = pl.BlockSpec(memory_space=pltpu.VMEM)


def shift(value, axis, by):
    n = lax.axis_size(axis)
    return lax.ppermute(value, axis, [(i, (i + by) % n) for i in range(n)])


def swap(value, axis):
    return lax.ppermute(value, axis, [(0, 1), (1, 0)])


def after(value, earlier):
    return lax.optimization_barrier((value, earlier))[0]


def spread(value, axis):
    n = lax.axis_size(axis)
    return lax.all_to_all(jnp.broadcast_to(value[None], (n,) + value.shape), axis, 0, 0, tiled=True)


def ring_copies(value, axis, n):
    return [value] + [shift(value, axis, s) for s in range(1, n)]


def column(row_ref, tokens):
    return jnp.transpose(jnp.broadcast_to(row_ref[0:1, :], (LANES, tokens)))


def logits_kernel(states, ids_ref, *refs):
    near, far = refs[0:3], refs[3:6]
    logits_ref, stats_ref, lab, xn, xf, wn, wf, digits, tops, picks, sems = refs[6:]
    tokens, cols = logits_ref.shape
    half, own = near[0].shape
    side = near[1].shape[1]
    started = []

    def copy(src, dst):
        c = pltpu.make_async_copy(src, dst, sems.at[len(started)])
        c.start()
        started.append(c)
        return c

    label = copy(states.at[:, pl.ds(2 * half, LANES)], digits)
    needs = [[] for _ in range(cols // WIDE)]
    for t in range(own // WIDE):
        c = pl.ds(t * WIDE, WIDE)
        if t == 0:
            needs[0].append(copy(states.at[:, pl.ds(0, half)], xn))
        needs[t].append(copy(near[0].at[:, c], wn.at[:, c]))
        if t == 0:
            needs[0].append(copy(states.at[:, pl.ds(half, half)], xf))
        needs[t].append(copy(far[0].at[:, c], wf.at[:, c]))
    for k in (1, 2):
        at = own + side * (k - 1)
        needs[at // WIDE].append(copy(near[k], wn.at[:, pl.ds(at, side)]))
        needs[at // WIDE].append(copy(far[k], wf.at[:, pl.ds(at, side)]))

    label.wait()
    v = digits[...].astype(F32)
    code = v[:, 0:1] + 256.0 * v[:, 1:2] + 65536.0 * v[:, 2:3]
    lab[...] = jnp.broadcast_to(code, (tokens, LANES)).astype(I32)

    for t in range(cols // WIDE):
        for c in needs[t]:
            c.wait()
        c = pl.ds(t * WIDE, WIDE)
        v = jnp.dot(xn[...], wn[:, c], preferred_element_type=F32) + jnp.dot(
            xf[...], wf[:, c], preferred_element_type=F32
        )
        logits_ref[:, c] = v
        top, picked = None, None
        for k in range(WIDE // LANES):
            part = v[:, k * LANES : (k + 1) * LANES]
            hit = ids_ref[0:1, pl.ds(t * WIDE + k * LANES, LANES)] == lab[...]
            mine = jnp.where(hit, part, 0.0)
            top = part if top is None else jnp.maximum(top, part)
            picked = mine if picked is None else picked + mine
        tops[...] = top if t == 0 else jnp.maximum(tops[...], top)
        picks[...] = picked if t == 0 else picks[...] + picked

    def chunk(k, _):
        r = pl.ds(pl.multiple_of(k * CHUNK, CHUNK), CHUNK)
        top = jnp.max(tops[r, :], axis=1, keepdims=True)
        total = jnp.sum(jnp.exp(logits_ref[r, :] - top), axis=1, keepdims=True)
        picked = jnp.sum(picks[r, :], axis=1, keepdims=True)
        lane = lax.broadcasted_iota(I32, (CHUNK, LANES), 1)
        tops[r, :] = jnp.where(lane == 0, top, jnp.where(lane == 1, total, picked))
        return 0

    lax.fori_loop(0, tokens // CHUNK, chunk, 0)
    stats_ref[...] = jnp.transpose(tops[...])[0:8, :]


def logits_call(states, ids, near, far):
    half = near[0].shape[0]
    tokens = states.shape[0]
    cols = ids.shape[1]
    return pl.pallas_call(
        logits_kernel,
        out_shape=(
            jax.ShapeDtypeStruct((tokens, cols), F32),
            jax.ShapeDtypeStruct((8, tokens), F32),
            jax.ShapeDtypeStruct((tokens, LANES), I32),
        ),
        in_specs=[ANY, VMEM] + [ANY] * 6,
        out_specs=(VMEM, VMEM, VMEM),
        scratch_shapes=[
            pltpu.VMEM((tokens, half), BF16),
            pltpu.VMEM((tokens, half), BF16),
            pltpu.VMEM((half, cols), BF16),
            pltpu.VMEM((half, cols), BF16),
            pltpu.VMEM((tokens, LANES), BF16),
            pltpu.VMEM((tokens, LANES), F32),
            pltpu.VMEM((tokens, LANES), F32),
            pltpu.SemaphoreType.DMA((32,)),
        ],
        compiler_params=pltpu.CompilerParams(vmem_limit_bytes=40 * MIB),
        cost_estimate=pl.CostEstimate(
            flops=4 * tokens * half * cols, bytes_accessed=20 * MIB, transcendentals=tokens * cols
        ),
        name="logits",
    )(states, ids, *near, *far)


def contract(slopes, w0, w1, w2):
    own, side = w0.shape[1], w1.shape[1]

    def nt(a, b):
        return lax.dot_general(a, b, (((1,), (1,)), ((), ())), preferred_element_type=F32)

    return (
        nt(slopes[:, 0:own], w0[...])
        + nt(slopes[:, own : own + side], w1[...])
        + nt(slopes[:, own + side :], w2[...])
    )


def pick_rows(at_ref, slopes_ref, near_rows, far_rows, steps):
    x, y = at_ref[0], at_ref[1]
    span = NY * PART
    for k, s in enumerate(steps):
        start = pl.multiple_of(((x + s) & 3) * span, span)
        near_rows[pl.ds(k * span, span), :] = slopes_ref[pl.ds(start, span), :]
        for a in range(NX):
            start = pl.multiple_of((a * NY + ((y + s) & 3)) * PART, PART)
            far_rows[pl.ds(k * span + a * PART, PART), :] = slopes_ref[pl.ds(start, PART), :]


def put_tile(outs, value, step):
    span = NY * PART
    for side in range(2):

        @pl.when(step // 2 == side)
        def _(side=side):
            for k in range(len(outs) // 2):
                outs[2 * k + side][...] = value[k * span : (k + 1) * span]


def ahead_kernel(at_ref, lab, ids_ref, lse_ref, logits_ref, *refs):
    near_w, far_w, near_out, far_out = refs[0:3], refs[3:6], refs[6:8], refs[8:10]
    slopes_ref, lse, near_rows, far_rows = refs[10:]
    tokens = logits_ref.shape[0]
    step = pl.program_id(0)

    @pl.when(step == 0)
    def _():
        lse[...] = column(lse_ref, tokens)

        def chunk(k, _):
            r = pl.ds(pl.multiple_of(k * CHUNK, CHUNK), CHUNK)
            hit = ids_ref[0:1, :] == lab[r, 0:1]
            p = jnp.exp(logits_ref[r, :] - lse[r, 0:1])
            slopes_ref[r, :] = (p - jnp.where(hit, 1.0, 0.0)).astype(BF16)
            return 0

        lax.fori_loop(0, tokens // CHUNK, chunk, 0)
        pick_rows(at_ref, slopes_ref, near_rows, far_rows, (2,))

    put_tile(near_out, contract(near_rows, *near_w), step)
    put_tile(far_out, contract(far_rows, *far_w), step)


def rest_kernel(at_ref, slopes_ref, *refs):
    near_w, far_w, near_out, far_out = refs[0:3], refs[3:6], refs[6:12], refs[12:18]
    near_rows, far_rows = refs[18:]
    step = pl.program_id(0)

    @pl.when(step == 0)
    def _():
        pick_rows(at_ref, slopes_ref, near_rows, far_rows, (1, 3, 0))

    put_tile(near_out, contract(near_rows, *near_w), step)
    put_tile(far_out, contract(far_rows, *far_w), step)


def product_call(kernel, heads, head_specs, weights, blocks, extra_out, extra_scratch, name):
    half = weights[0].shape[0]
    cols = sum(w.shape[1] for w in weights) // 2
    span = NY * PART
    part = jax.ShapeDtypeStruct((span, half // 2), F32)
    left = pl.BlockSpec((span, TILE), lambda g: (0, jnp.minimum(g, 1)))
    right = pl.BlockSpec((span, TILE), lambda g: (0, jnp.maximum(g - 2, 0)))
    rows = pltpu.VMEM((blocks * span, cols), BF16)
    return pl.pallas_call(
        kernel,
        grid=(half // TILE,),
        out_shape=tuple([part] * (4 * blocks) + extra_out),
        in_specs=head_specs + [pl.BlockSpec((TILE, w.shape[1]), lambda g: (g, 0)) for w in weights],
        out_specs=tuple([left, right] * (2 * blocks) + [whole_block(e.shape) for e in extra_out]),
        scratch_shapes=extra_scratch + [rows, rows],
        compiler_params=pltpu.CompilerParams(vmem_limit_bytes=40 * MIB),
        cost_estimate=pl.CostEstimate(
            flops=4 * blocks * span * half * cols, bytes_accessed=16 * MIB, transcendentals=0
        ),
        name=name,
    )(*heads, *weights)


def whole_block(shape):
    return pl.BlockSpec(shape, lambda g: (0,) * len(shape))


def assemble_kernel(at_ref, own0, own1, other0, other1, out, sems):
    z4, z2 = at_ref[2], at_ref[3]
    up = (z4 + z2) & 3
    down = (z4 + z2 + 3) & 3
    copies = []
    for core, (src, parity, base) in enumerate(
        ((own0, z2, z4), (own1, z2, z4), (other0, 1 - z2, up), (other1, 1 - z2, down))
    ):
        for k in range(NZ4):
            copies.append(
                pltpu.make_async_copy(
                    src.at[k], out.at[core % 2, parity, (base - k) & 3], sems.at[core * NZ4 + k]
                )
            )
    for c in copies:
        c.start()
    for c in copies:
        c.wait()


def assemble_call(at, own0, own1, other0, other1):
    half = own0.shape[-1]
    return pl.pallas_call(
        assemble_kernel,
        out_shape=jax.ShapeDtypeStruct((2, NZ2, NZ4, QUARTER, half), F32),
        in_specs=[SMEM] + [ANY] * 4,
        out_specs=ANY,
        scratch_shapes=[pltpu.SemaphoreType.DMA((4 * NZ4,))],
        compiler_params=pltpu.CompilerParams(vmem_limit_bytes=40 * MIB),
        name="assemble",
    )(at, own0, own1, other0, other1)


def per_device(hidden_state, weight, targets):
    d = lax.axis_index("depth")
    z2 = lax.axis_index("z2")
    z4 = lax.axis_index("z4")
    x = lax.axis_index("x")
    y = lax.axis_index("y")
    z = z4 * NZ2 + z2
    nz = NZ4 * NZ2
    cols = weight.shape[1]
    side = cols // 2
    half = hidden_state.shape[1]
    tokens = NROW * PART
    at = jnp.stack([x, y, z4, z2]).astype(I32)

    near = lax.dynamic_slice(hidden_state, ((2 * d + z2) * PART, 0), (PART, half))
    far = swap(lax.dynamic_slice(hidden_state, ((2 * (1 - d) + z2) * PART, 0), (PART, half)), "depth")
    label = lax.dynamic_slice(targets, ((2 * d + z2) * PART,), (PART,))
    digits = jnp.stack([label % 256, (label // 256) % 256, label // 65536], axis=1).astype(BF16)
    wide = jnp.concatenate([near, far, jnp.pad(digits, ((0, 0), (0, LANES - 3)))], axis=1)
    states = lax.all_gather(wide, ROW, axis=0, tiled=True)

    from_next = shift(weight[:, :side], Z, -1)
    from_prev = shift(weight[:, side:], Z, 1)

    blocks = [weight, from_next, from_prev]
    others = [swap(b, "depth") for b in blocks]
    first = (x * NY + y) * nz
    starts = [
        (first + z) * cols,
        (first + (z + 1) % nz) * cols,
        (first + (z + nz - 1) % nz) * cols + side,
    ]
    ids = jnp.concatenate([s + jnp.arange(b.shape[1], dtype=I32) for s, b in zip(starts, blocks)])
    ids = jnp.broadcast_to(ids[None], (8, ids.shape[0]))

    logits, stats, labels = logits_call(states, ids, blocks, others)
    top, total, picked = stats[0], stats[1], stats[2]
    for axis in (ROW, "z4"):
        stats = spread(jnp.stack([top, total, picked]), axis)
        tops, totals, pickeds = stats[:, 0], stats[:, 1], stats[:, 2]
        top = tops.max(axis=0)
        total = jnp.sum(totals * jnp.exp(tops - top[None]), axis=0)
        picked = jnp.sum(pickeds, axis=0)
    lse = top + jnp.log(total)

    token_loss = lax.dynamic_slice((lse - picked).reshape(NROW, PART), (x * NY + y, 0), (1, PART)).reshape(PART)
    loss_pair = jnp.stack([token_loss, swap(token_loss, "z2")])
    loss = jnp.where(z2 == 0, loss_pair, loss_pair[::-1]).reshape(2 * PART)

    row_spec = whole_block((8, tokens))
    *two, slopes = product_call(
        ahead_kernel,
        [at, labels, ids, jnp.broadcast_to(lse[None], (8, tokens)), logits],
        [SMEM, whole_block(labels.shape), whole_block(ids.shape), row_spec, whole_block(logits.shape)],
        blocks + others,
        1,
        [jax.ShapeDtypeStruct(logits.shape, BF16)],
        [pltpu.VMEM((tokens, LANES), F32)],
        "ahead",
    )
    rest = product_call(
        rest_kernel, [at, slopes], [SMEM, whole_block(slopes.shape)], blocks + others, 3, [], [], "rest"
    )

    passed = [shift(t, ax, by) for t, (ax, by) in zip(two, (("x", 1), ("x", -1), ("y", 1), ("y", -1)))]
    rest = lax.optimization_barrier((tuple(rest), tuple(passed)))[0]

    def first_stage(parts, from_back, from_ahead, axis):
        next_left, next_right, last_left, last_right, own_left, own_right = parts
        right_1 = shift(next_right, axis, 1)
        left_1 = shift(last_left, axis, -1)
        left_2 = shift(after(next_left + from_back, right_1), axis, 1)
        right_2 = shift(after(last_right + from_ahead, left_1), axis, -1)
        return jnp.concatenate([own_left + left_1 + left_2, own_right + right_1 + right_2], axis=1)

    def ring_sum(parts, axis):
        terms = [parts[0]] + [shift(p, axis, s) for s, p in enumerate(parts) if s]
        return terms[0] + terms[1] + terms[2] + terms[3]

    near_x = first_stage(rest[0:6], passed[0], passed[1], "x").reshape(NY, PART, half)
    far_y = first_stage(rest[6:12], passed[2], passed[3], "y").reshape(NX, PART, half)
    near_grad = ring_sum([lax.dynamic_index_in_dim(near_x, (y + s) % NY, 0, False) for s in range(NY)], "y")
    far_grad = ring_sum([lax.dynamic_index_in_dim(far_y, (x + s) % NX, 0, False) for s in range(NX)], "x")
    crossed = swap(far_grad, "depth")
    pair = jnp.stack([near_grad, crossed])
    pair = jnp.where(d == 0, pair, pair[::-1]).reshape(2, NZ4, QUARTER, half)
    done = ring_sum([lax.dynamic_index_in_dim(pair, (z4 + s) % NZ4, 1, False) for s in range(NZ4)], "z4")
    copies = ring_copies(done, "z4", NZ4)
    own0 = jnp.stack([c[0] for c in copies])
    own1 = jnp.stack([c[1] for c in copies])
    other0 = shift(own0, Z, -1)
    other1 = shift(own1, Z, 1)
    grad = assemble_call(at, own0, own1, other0, other1).reshape(4 * PART, half)
    return loss, grad


def solution(mesh):
    fine = Mesh(mesh.devices.reshape(NX, NY, NZ4, NZ2, 2), ("x", "y", "z4", "z2", "depth"))
    return jax.shard_map(
        per_device,
        mesh=fine,
        in_specs=(P(ROW, "depth"), P("depth", ROW + Z), P(ROW)),
        out_specs=(P(ROW + ("depth",)), P(ROW, "depth")),
        check_vma=False,
    )
```

```python
import functools

import jax
import jax.numpy as jnp
from jax import lax
from jax.experimental import pallas as pl
from jax.experimental.pallas import tpu as pltpu
from jax.sharding import Mesh, PartitionSpec as P

F32 = jnp.float32
BF16 = jnp.bfloat16
I32 = jnp.int32
ROW = ("x", "y")
Z = ("z4", "z2")
NX, NY, NZ4, NZ2 = 4, 4, 4, 2
NROW = NX * NY
PART = 32
QUARTER = PART // NZ4
LANES = 128
CHUNK = 32
WIDE = 768
TILE = 512
MIB = 1024 * 1024
ANY = pl.BlockSpec(memory_space=pl.ANY)
SMEM = pl.BlockSpec(memory_space=pltpu.SMEM)
VMEM = pl.BlockSpec(memory_space=pltpu.VMEM)


def shift(value, axis, by):
    n = lax.axis_size(axis)
    return lax.ppermute(value, axis, [(i, (i + by) % n) for i in range(n)])


def swap(value, axis):
    return lax.ppermute(value, axis, [(0, 1), (1, 0)])


def after(value, earlier):
    return lax.optimization_barrier((value, earlier))[0]


def spread(value, axis):
    n = lax.axis_size(axis)
    return lax.all_to_all(jnp.broadcast_to(value[None], (n,) + value.shape), axis, 0, 0, tiled=True)


def ring_copies(value, axis, n):
    return [value] + [shift(value, axis, s) for s in range(1, n)]


def column(row_ref, tokens):
    return jnp.transpose(jnp.broadcast_to(row_ref[0:1, :], (LANES, tokens)))


def logits_kernel(states, ids_ref, *refs):
    near, far = refs[0:3], refs[3:6]
    logits_ref, stats_ref, lab, xn, xf, wn, wf, digits, tops, sums, picks, sems = refs[6:]
    tokens, cols = logits_ref.shape
    half, own = near[0].shape
    side = near[1].shape[1]
    count = [0]

    def copy(src, dst):
        count[0] += 1
        return pltpu.make_async_copy(src, dst, sems.at[count[0] - 1])

    label = copy(states.at[:, pl.ds(2 * half, LANES)], digits)
    sides = [pl.ds(own, side), pl.ds(own + side, side)]
    needs = [
        [copy(states.at[:, pl.ds(0, half)], xn), copy(near[0], wn.at[:, pl.ds(0, own)])],
        [copy(states.at[:, pl.ds(half, half)], xf), copy(far[0], wf.at[:, pl.ds(0, own)])],
        [copy(near[k + 1], wn.at[:, sides[k]]) for k in range(2)],
        [copy(far[k + 1], wf.at[:, sides[k]]) for k in range(2)],
    ]

    def start(t):
        for c in needs[t] if t < len(needs) else []:
            c.start()

    label.start()
    start(0)
    start(1)
    label.wait()
    v = digits[...].astype(F32)
    code = v[:, 0:1] + 256.0 * v[:, 1:2] + 65536.0 * v[:, 2:3]
    lab[...] = jnp.broadcast_to(code, (tokens, LANES)).astype(I32)

    for t in range(cols // WIDE):
        c = pl.ds(t * WIDE, WIDE)
        for k in (2 * t, 2 * t + 1):
            for copied in needs[k]:
                copied.wait()
            start(k + 2)
            if k % 2 == 0:
                logits_ref[:, c] = jnp.dot(xn[...], wn[:, c], preferred_element_type=F32)
        v = logits_ref[:, c] + jnp.dot(xf[...], wf[:, c], preferred_element_type=F32)
        logits_ref[:, c] = v
        parts = [v[:, k * LANES : (k + 1) * LANES] for k in range(WIDE // LANES)]
        top = functools.reduce(jnp.maximum, parts)
        if t:
            top = jnp.maximum(tops[...], top)
        total = sum(jnp.exp(p - top) for p in parts)
        picked = None
        for k, p in enumerate(parts):
            hit = ids_ref[0:1, pl.ds(t * WIDE + k * LANES, LANES)] == lab[...]
            mine = jnp.where(hit, p, 0.0)
            picked = mine if picked is None else picked + mine
        sums[...] = total + sums[...] * jnp.exp(tops[...] - top) if t else total
        picks[...] = picks[...] + picked if t else picked
        tops[...] = top

    top = jnp.max(tops[...], axis=1, keepdims=True)
    total = jnp.sum(sums[...] * jnp.exp(tops[...] - top), axis=1, keepdims=True)
    picked = jnp.sum(picks[...], axis=1, keepdims=True)
    lane = lax.broadcasted_iota(I32, (tokens, LANES), 1)
    packed = jnp.where(lane == 0, top, jnp.where(lane == 1, total, picked))
    stats_ref[...] = jnp.transpose(packed)[0:8, :]


def logits_call(states, ids, near, far):
    half = near[0].shape[0]
    tokens = states.shape[0]
    cols = ids.shape[1]
    return pl.pallas_call(
        logits_kernel,
        out_shape=(
            jax.ShapeDtypeStruct((tokens, cols), F32),
            jax.ShapeDtypeStruct((8, tokens), F32),
            jax.ShapeDtypeStruct((tokens, LANES), I32),
        ),
        in_specs=[ANY, VMEM] + [ANY] * 6,
        out_specs=(VMEM, VMEM, VMEM),
        scratch_shapes=[
            pltpu.VMEM((tokens, half), BF16),
            pltpu.VMEM((tokens, half), BF16),
            pltpu.VMEM((half, cols), BF16),
            pltpu.VMEM((half, cols), BF16),
            pltpu.VMEM((tokens, LANES), BF16),
            pltpu.VMEM((tokens, LANES), F32),
            pltpu.VMEM((tokens, LANES), F32),
            pltpu.VMEM((tokens, LANES), F32),
            pltpu.SemaphoreType.DMA((32,)),
        ],
        compiler_params=pltpu.CompilerParams(vmem_limit_bytes=28 * MIB),
        cost_estimate=pl.CostEstimate(
            flops=4 * tokens * half * cols, bytes_accessed=20 * MIB, transcendentals=tokens * cols
        ),
        name="logits",
    )(states, ids, *near, *far)


def contract(slopes_ref, w0, w1, w2, first=0, last=None):
    own, side = w0.shape[1], w1.shape[1]
    slopes = slopes_ref[first:last, :]

    def nt(a, b):
        return lax.dot_general(a, b, (((1,), (1,)), ((), ())), preferred_element_type=F32)

    return (
        nt(slopes[:, 0:own], w0[...])
        + nt(slopes[:, own : own + side], w1[...])
        + nt(slopes[:, own + side :], w2[...])
    )


def pick_rows(at_ref, slopes_ref, near_rows, far_rows, steps):
    x, y = at_ref[0], at_ref[1]
    span = NY * PART
    for k, s in enumerate(steps):
        start = pl.multiple_of(((x + s) & 3) * span, span)
        near_rows[pl.ds(k * span, span), :] = slopes_ref[pl.ds(start, span), :]
        for a in range(NX):
            start = pl.multiple_of((a * NY + ((y + s) & 3)) * PART, PART)
            far_rows[pl.ds(k * span + a * PART, PART), :] = slopes_ref[pl.ds(start, PART), :]


def ahead_kernel(at_ref, lab, ids_ref, lse_ref, logits_ref, *refs):
    near_w, far_w, near_out, far_out = refs[0:3], refs[3:6], refs[6:8], refs[8:10]
    slopes_ref, lse, near_rows, far_rows = refs[10:]
    tokens = logits_ref.shape[0]
    step = pl.program_id(0)

    @pl.when(step == 0)
    def _():
        lse[...] = column(lse_ref, tokens)

        def chunk(k, _):
            r = pl.ds(pl.multiple_of(k * CHUNK, CHUNK), CHUNK)
            hit = ids_ref[0:1, :] == lab[r, 0:1]
            p = jnp.exp(logits_ref[r, :] - lse[r, 0:1])
            slopes_ref[r, :] = (p - jnp.where(hit, 1.0, 0.0)).astype(BF16)
            return 0

        lax.fori_loop(0, tokens // CHUNK, chunk, 0)
        pick_rows(at_ref, slopes_ref, near_rows, far_rows, (2,))

    near_v, far_v = contract(near_rows, *near_w), contract(far_rows, *far_w)
    for side in range(2):

        @pl.when(step // 2 == side)
        def _(side=side):
            near_out[side][...] = near_v
            far_out[side][...] = far_v


def beside_kernel(at_ref, slopes_ref, *refs):
    near_w, far_w, near_out, far_out = refs[0:3], refs[3:6], refs[6:8], refs[8:10]
    near_rows, far_rows = refs[10:]
    step = pl.program_id(0)
    span = NY * PART

    @pl.when(step == 0)
    def _():
        pick_rows(at_ref, slopes_ref, near_rows, far_rows, (3, 1))

    for side in range(2):

        @pl.when(step // 2 == side)
        def _(side=side):
            at = (side * span, (side + 1) * span)
            near_out[side][...] = contract(near_rows, *near_w, *at)
            far_out[side][...] = contract(far_rows, *far_w, *at)


def onward_kernel(at_ref, slopes_ref, *refs):
    near_w, far_w, near_in, far_in = refs[0:3], refs[3:6], refs[6:8], refs[8:10]
    near_out, far_out = refs[10:14], refs[14:18]
    near_rows, far_rows = refs[18:]
    step = pl.program_id(0)
    span = NY * PART

    @pl.when(step == 0)
    def _():
        pick_rows(at_ref, slopes_ref, near_rows, far_rows, (1, 0, 3))

    for side in range(2):

        @pl.when(step // 2 == side)
        def _(side=side):
            for rows, w, came, out in ((near_rows, near_w, near_in, near_out), (far_rows, far_w, far_in, far_out)):
                v = contract(rows, *w, side * span, (side + 2) * span)
                sent = v[side * span : (side + 1) * span]
                out[side][...] = sent + came[side][...]
                out[2 + side][...] = v[(1 - side) * span : (2 - side) * span]


def product_call(kernel, heads, weights, blocks, outs, came=(), extra_out=(), extra_scratch=(), name=None):
    half = weights[0].shape[0]
    cols = sum(w.shape[1] for w in weights) // 2
    span = NY * PART
    part = jax.ShapeDtypeStruct((span, half // 2), F32)
    left = pl.BlockSpec((span, TILE), lambda g: (0, jnp.minimum(g, 1)))
    right = pl.BlockSpec((span, TILE), lambda g: (0, jnp.maximum(g - 2, 0)))
    rows = pltpu.VMEM((blocks * span, cols), BF16)
    return pl.pallas_call(
        kernel,
        grid=(half // TILE,),
        out_shape=tuple([part] * outs + list(extra_out)),
        in_specs=[SMEM]
        + [whole_block(h.shape) for h in heads[1:]]
        + [pl.BlockSpec((TILE, w.shape[1]), lambda g: (g, 0)) for w in weights]
        + [left, right] * (len(came) // 2),
        out_specs=tuple([left, right] * (outs // 2) + [whole_block(e.shape) for e in extra_out]),
        scratch_shapes=list(extra_scratch) + [rows, rows],
        compiler_params=pltpu.CompilerParams(vmem_limit_bytes=24 * MIB),
        cost_estimate=pl.CostEstimate(
            flops=outs * span * half * cols, bytes_accessed=16 * MIB, transcendentals=0
        ),
        name=name,
    )(*heads, *weights, *came)


def whole_block(shape):
    return pl.BlockSpec(shape, lambda g: (0,) * len(shape))


def assemble_kernel(at_ref, own0, own1, other0, other1, out, sems):
    z4, z2 = at_ref[2], at_ref[3]
    up = (z4 + z2) & 3
    down = (z4 + z2 + 3) & 3
    copies = []
    for core, (src, parity, base) in enumerate(
        ((own0, z2, z4), (own1, z2, z4), (other0, 1 - z2, up), (other1, 1 - z2, down))
    ):
        for k in range(NZ4):
            copies.append(
                pltpu.make_async_copy(
                    src.at[k], out.at[core % 2, parity, (base - k) & 3], sems.at[core * NZ4 + k]
                )
            )
    for c in copies:
        c.start()
    for c in copies:
        c.wait()


def assemble_call(at, own0, own1, other0, other1):
    half = own0.shape[-1]
    return pl.pallas_call(
        assemble_kernel,
        out_shape=jax.ShapeDtypeStruct((2, NZ2, NZ4, QUARTER, half), F32),
        in_specs=[SMEM] + [ANY] * 4,
        out_specs=ANY,
        scratch_shapes=[pltpu.SemaphoreType.DMA((4 * NZ4,))],
        compiler_params=pltpu.CompilerParams(vmem_limit_bytes=24 * MIB),
        name="assemble",
    )(at, own0, own1, other0, other1)


def per_device(hidden_state, weight, targets):
    d = lax.axis_index("depth")
    z2 = lax.axis_index("z2")
    z4 = lax.axis_index("z4")
    x = lax.axis_index("x")
    y = lax.axis_index("y")
    z = z4 * NZ2 + z2
    nz = NZ4 * NZ2
    cols = weight.shape[1]
    side = cols // 2
    half = hidden_state.shape[1]
    tokens = NROW * PART
    at = jnp.stack([x, y, z4, z2]).astype(I32)

    near = lax.dynamic_slice(hidden_state, ((2 * d + z2) * PART, 0), (PART, half))
    far = swap(lax.dynamic_slice(hidden_state, ((2 * (1 - d) + z2) * PART, 0), (PART, half)), "depth")
    label = lax.dynamic_slice(targets, ((2 * d + z2) * PART,), (PART,))
    digits = jnp.stack([label % 256, (label // 256) % 256, label // 65536], axis=1).astype(BF16)
    wide = jnp.concatenate([near, far, jnp.pad(digits, ((0, 0), (0, LANES - 3)))], axis=1)
    states = lax.all_gather(wide, ROW, axis=0, tiled=True)

    from_next = shift(weight[:, :side], Z, -1)
    from_prev = shift(weight[:, side:], Z, 1)

    blocks = [weight, from_next, from_prev]
    others = [swap(b, "depth") for b in blocks]
    first = (x * NY + y) * nz
    starts = [
        (first + z) * cols,
        (first + (z + 1) % nz) * cols,
        (first + (z + nz - 1) % nz) * cols + side,
    ]
    ids = jnp.concatenate([s + jnp.arange(b.shape[1], dtype=I32) for s, b in zip(starts, blocks)])
    ids = jnp.broadcast_to(ids[None], (8, ids.shape[0]))

    logits, stats, labels = logits_call(states, ids, blocks, others)
    top, total, picked = stats[0], stats[1], stats[2]
    for axis in (ROW, "z4"):
        stats = spread(jnp.stack([top, total, picked]), axis)
        tops, totals, pickeds = stats[:, 0], stats[:, 1], stats[:, 2]
        top = tops.max(axis=0)
        total = jnp.sum(totals * jnp.exp(tops - top[None]), axis=0)
        picked = jnp.sum(pickeds, axis=0)
    lse = top + jnp.log(total)

    token_loss = lax.dynamic_slice((lse - picked).reshape(NROW, PART), (x * NY + y, 0), (1, PART)).reshape(PART)
    loss_pair = jnp.stack([token_loss, swap(token_loss, "z2")])
    loss = jnp.where(z2 == 0, loss_pair, loss_pair[::-1]).reshape(2 * PART)

    *two, slopes = product_call(
        ahead_kernel,
        [at, labels, ids, jnp.broadcast_to(lse[None], (8, tokens)), logits],
        blocks + others,
        1,
        4,
        extra_out=[jax.ShapeDtypeStruct(logits.shape, BF16)],
        extra_scratch=[pltpu.VMEM((tokens, LANES), F32)],
        name="ahead",
    )

    links = (("x", 1), ("x", -1), ("y", 1), ("y", -1))
    passed = [shift(t, ax, by) for t, (ax, by) in zip(two, links)]
    beside = product_call(beside_kernel, [at, slopes], blocks + others, 2, 4, name="beside")
    straight = [shift(t, ax, -by) for t, (ax, by) in zip(beside, links)]
    onward = product_call(onward_kernel, [at, slopes], blocks + others, 3, 8, came=passed, name="onward")

    def first_stage(sums, straight, links):
        last = [shift(after(t, s), ax, by) for t, s, (ax, by) in zip(sums[:2], reversed(straight), links)]
        return jnp.concatenate([o + s + l for o, s, l in zip(sums[2:], straight, last)], axis=1)

    near_x = first_stage(onward[0:4], straight[0:2], links[:2]).reshape(NY, PART, half)
    far_y = first_stage(onward[4:8], straight[2:4], links[2:]).reshape(NX, PART, half)

    def ring_sum(parts, axis):
        terms = [parts[0]] + [shift(p, axis, s) for s, p in enumerate(parts) if s]
        return terms[0] + terms[1] + terms[2] + terms[3]

    near_grad = ring_sum([lax.dynamic_index_in_dim(near_x, (y + s) % NY, 0, False) for s in range(NY)], "y")
    far_grad = ring_sum([lax.dynamic_index_in_dim(far_y, (x + s) % NX, 0, False) for s in range(NX)], "x")
    crossed = swap(far_grad, "depth")
    pair = jnp.stack([near_grad, crossed])
    pair = jnp.where(d == 0, pair, pair[::-1]).reshape(2, NZ4, QUARTER, half)
    done = ring_sum([lax.dynamic_index_in_dim(pair, (z4 + s) % NZ4, 1, False) for s in range(NZ4)], "z4")
    copies = ring_copies(done, "z4", NZ4)
    own0 = jnp.stack([c[0] for c in copies])
    own1 = jnp.stack([c[1] for c in copies])
    other0 = shift(own0, Z, -1)
    other1 = shift(own1, Z, 1)
    grad = assemble_call(at, own0, own1, other0, other1).reshape(4 * PART, half)
    return loss, grad


def solution(mesh):
    fine = Mesh(mesh.devices.reshape(NX, NY, NZ4, NZ2, 2), ("x", "y", "z4", "z2", "depth"))
    return jax.shard_map(
        per_device,
        mesh=fine,
        in_specs=(P(ROW, "depth"), P("depth", ROW + Z), P(ROW)),
        out_specs=(P(ROW + ("depth",)), P(ROW, "depth")),
        check_vma=False,
    )
```

```python
import functools

import jax
import jax.numpy as jnp
from jax import lax
from jax.experimental import pallas as pl
from jax.experimental.pallas import tpu as pltpu
from jax.sharding import Mesh, PartitionSpec as P

F32 = jnp.float32
BF16 = jnp.bfloat16
I32 = jnp.int32
ROW = ("x", "y")
Z = ("z4", "z2")
NX, NY, NZ4, NZ2 = 4, 4, 4, 2
NROW = NX * NY
PART = 32
QUARTER = PART // NZ4
LANES = 128
CHUNK = 32
WIDE = 768
TILE = 512
MIB = 1024 * 1024
ANY = pl.BlockSpec(memory_space=pl.ANY)
SMEM = pl.BlockSpec(memory_space=pltpu.SMEM)
VMEM = pl.BlockSpec(memory_space=pltpu.VMEM)


def shift(value, axis, by):
    n = lax.axis_size(axis)
    return lax.ppermute(value, axis, [(i, (i + by) % n) for i in range(n)])


def swap(value, axis):
    return lax.ppermute(value, axis, [(0, 1), (1, 0)])


def after(value, earlier):
    return lax.optimization_barrier((value, earlier))[0]


def spread(value, axis):
    n = lax.axis_size(axis)
    return lax.all_to_all(jnp.broadcast_to(value[None], (n,) + value.shape), axis, 0, 0, tiled=True)


def ring_copies(value, axis, n):
    return [value] + [shift(value, axis, s) for s in range(1, n)]


def column(row_ref, tokens):
    return jnp.transpose(jnp.broadcast_to(row_ref[0:1, :], (LANES, tokens)))


def logits_kernel(states, ids_ref, *refs):
    near, far = refs[0:3], refs[3:6]
    logits_ref, stats_ref, lab, xn, xf, wn, wf, digits, tops, sums, picks, sems = refs[6:]
    tokens, cols = logits_ref.shape
    half, own = near[0].shape
    side = near[1].shape[1]
    count = [0]

    def copy(src, dst):
        count[0] += 1
        return pltpu.make_async_copy(src, dst, sems.at[count[0] - 1])

    label = copy(states.at[:, pl.ds(2 * half, LANES)], digits)
    sides = [pl.ds(own, side), pl.ds(own + side, side)]
    needs = [
        [copy(states.at[:, pl.ds(0, half)], xn), copy(near[0], wn.at[:, pl.ds(0, own)])],
        [copy(states.at[:, pl.ds(half, half)], xf), copy(far[0], wf.at[:, pl.ds(0, own)])],
        [copy(near[k + 1], wn.at[:, sides[k]]) for k in range(2)],
        [copy(far[k + 1], wf.at[:, sides[k]]) for k in range(2)],
    ]

    def start(t):
        for c in needs[t] if t < len(needs) else []:
            c.start()

    label.start()
    start(0)
    start(1)
    label.wait()
    v = digits[...].astype(F32)
    code = v[:, 0:1] + 256.0 * v[:, 1:2] + 65536.0 * v[:, 2:3]
    lab[...] = jnp.broadcast_to(code, (tokens, LANES)).astype(I32)

    for t in range(cols // WIDE):
        c = pl.ds(t * WIDE, WIDE)
        for k in (2 * t, 2 * t + 1):
            for copied in needs[k]:
                copied.wait()
            start(k + 2)
            if k % 2 == 0:
                logits_ref[:, c] = jnp.dot(xn[...], wn[:, c], preferred_element_type=F32)
        v = logits_ref[:, c] + jnp.dot(xf[...], wf[:, c], preferred_element_type=F32)
        logits_ref[:, c] = v
        parts = [v[:, k * LANES : (k + 1) * LANES] for k in range(WIDE // LANES)]
        top = functools.reduce(jnp.maximum, parts)
        if t:
            top = jnp.maximum(tops[...], top)
        total = sum(jnp.exp(p - top) for p in parts)
        picked = None
        for k, p in enumerate(parts):
            hit = ids_ref[0:1, pl.ds(t * WIDE + k * LANES, LANES)] == lab[...]
            mine = jnp.where(hit, p, 0.0)
            picked = mine if picked is None else picked + mine
        sums[...] = total + sums[...] * jnp.exp(tops[...] - top) if t else total
        picks[...] = picks[...] + picked if t else picked
        tops[...] = top

    top = jnp.max(tops[...], axis=1, keepdims=True)
    total = jnp.sum(sums[...] * jnp.exp(tops[...] - top), axis=1, keepdims=True)
    picked = jnp.sum(picks[...], axis=1, keepdims=True)
    lane = lax.broadcasted_iota(I32, (tokens, LANES), 1)
    packed = jnp.where(lane == 0, top, jnp.where(lane == 1, total, picked))
    stats_ref[...] = jnp.transpose(packed)[0:8, :]


def logits_call(states, ids, near, far):
    half = near[0].shape[0]
    tokens = states.shape[0]
    cols = ids.shape[1]
    return pl.pallas_call(
        logits_kernel,
        out_shape=(
            jax.ShapeDtypeStruct((tokens, cols), F32),
            jax.ShapeDtypeStruct((8, tokens), F32),
            jax.ShapeDtypeStruct((tokens, LANES), I32),
        ),
        in_specs=[ANY, VMEM] + [ANY] * 6,
        out_specs=(VMEM, VMEM, VMEM),
        scratch_shapes=[
            pltpu.VMEM((tokens, half), BF16),
            pltpu.VMEM((tokens, half), BF16),
            pltpu.VMEM((half, cols), BF16),
            pltpu.VMEM((half, cols), BF16),
            pltpu.VMEM((tokens, LANES), BF16),
            pltpu.VMEM((tokens, LANES), F32),
            pltpu.VMEM((tokens, LANES), F32),
            pltpu.VMEM((tokens, LANES), F32),
            pltpu.SemaphoreType.DMA((32,)),
        ],
        compiler_params=pltpu.CompilerParams(vmem_limit_bytes=56 * MIB),
        cost_estimate=pl.CostEstimate(
            flops=4 * tokens * half * cols, bytes_accessed=20 * MIB, transcendentals=tokens * cols
        ),
        name="logits",
    )(states, ids, *near, *far)


def contract(slopes_ref, w0, w1, w2, first=0, last=None):
    own, side = w0.shape[1], w1.shape[1]
    slopes = slopes_ref[first:last, :]

    def nt(a, b):
        return lax.dot_general(a, b, (((1,), (1,)), ((), ())), preferred_element_type=F32)

    return (
        nt(slopes[:, 0:own], w0[...])
        + nt(slopes[:, own : own + side], w1[...])
        + nt(slopes[:, own + side :], w2[...])
    )


def pick_rows(at_ref, slopes_ref, near_rows, far_rows, steps):
    x, y = at_ref[0], at_ref[1]
    span = NY * PART
    for k, s in enumerate(steps):
        start = pl.multiple_of(((x + s) & 3) * span, span)
        near_rows[pl.ds(k * span, span), :] = slopes_ref[pl.ds(start, span), :]
        for a in range(NX):
            start = pl.multiple_of((a * NY + ((y + s) & 3)) * PART, PART)
            far_rows[pl.ds(k * span + a * PART, PART), :] = slopes_ref[pl.ds(start, PART), :]


def ahead_kernel(at_ref, lab, ids_ref, lse_ref, logits_ref, *refs):
    near_w, far_w, near_out, far_out = refs[0:3], refs[3:6], refs[6:8], refs[8:10]
    slopes_ref, lse, near_rows, far_rows = refs[10:]
    tokens = logits_ref.shape[0]
    step = pl.program_id(0)

    @pl.when(step == 0)
    def _():
        lse[...] = column(lse_ref, tokens)

        def chunk(k, _):
            r = pl.ds(pl.multiple_of(k * CHUNK, CHUNK), CHUNK)
            hit = ids_ref[0:1, :] == lab[r, 0:1]
            p = jnp.exp(logits_ref[r, :] - lse[r, 0:1])
            slopes_ref[r, :] = (p - jnp.where(hit, 1.0, 0.0)).astype(BF16)
            return 0

        lax.fori_loop(0, tokens // CHUNK, chunk, 0)
        pick_rows(at_ref, slopes_ref, near_rows, far_rows, (2,))

    near_v, far_v = contract(near_rows, *near_w), contract(far_rows, *far_w)
    for side in range(2):

        @pl.when(step // 2 == side)
        def _(side=side):
            near_out[side][...] = near_v
            far_out[side][...] = far_v


def beside_kernel(at_ref, slopes_ref, *refs):
    near_w, far_w, near_out, far_out = refs[0:3], refs[3:6], refs[6:8], refs[8:10]
    near_rows, far_rows = refs[10:]
    step = pl.program_id(0)
    span = NY * PART

    @pl.when(step == 0)
    def _():
        pick_rows(at_ref, slopes_ref, near_rows, far_rows, (3, 1))

    for side in range(2):

        @pl.when(step // 2 == side)
        def _(side=side):
            at = (side * span, (side + 1) * span)
            near_out[side][...] = contract(near_rows, *near_w, *at)
            far_out[side][...] = contract(far_rows, *far_w, *at)


def onward_kernel(at_ref, slopes_ref, *refs):
    near_w, far_w, near_in, far_in = refs[0:3], refs[3:6], refs[6:8], refs[8:10]
    near_out, far_out = refs[10:14], refs[14:18]
    near_rows, far_rows = refs[18:]
    step = pl.program_id(0)
    span = NY * PART

    @pl.when(step == 0)
    def _():
        pick_rows(at_ref, slopes_ref, near_rows, far_rows, (1, 0, 3))

    for side in range(2):

        @pl.when(step // 2 == side)
        def _(side=side):
            for rows, w, came, out in ((near_rows, near_w, near_in, near_out), (far_rows, far_w, far_in, far_out)):
                v = contract(rows, *w, side * span, (side + 2) * span)
                sent = v[side * span : (side + 1) * span]
                out[side][...] = sent + came[side][...]
                out[2 + side][...] = v[(1 - side) * span : (2 - side) * span]


def product_call(kernel, heads, weights, blocks, outs, came=(), extra_out=(), extra_scratch=(), name=None):
    half = weights[0].shape[0]
    cols = sum(w.shape[1] for w in weights) // 2
    span = NY * PART
    part = jax.ShapeDtypeStruct((span, half // 2), F32)
    left = pl.BlockSpec((span, TILE), lambda g: (0, jnp.minimum(g, 1)))
    right = pl.BlockSpec((span, TILE), lambda g: (0, jnp.maximum(g - 2, 0)))
    rows = pltpu.VMEM((blocks * span, cols), BF16)
    return pl.pallas_call(
        kernel,
        grid=(half // TILE,),
        out_shape=tuple([part] * outs + list(extra_out)),
        in_specs=[SMEM]
        + [whole_block(h.shape) for h in heads[1:]]
        + [pl.BlockSpec((TILE, w.shape[1]), lambda g: (g, 0)) for w in weights]
        + [left, right] * (len(came) // 2),
        out_specs=tuple([left, right] * (outs // 2) + [whole_block(e.shape) for e in extra_out]),
        scratch_shapes=list(extra_scratch) + [rows, rows],
        compiler_params=pltpu.CompilerParams(vmem_limit_bytes=56 * MIB),
        cost_estimate=pl.CostEstimate(
            flops=outs * span * half * cols, bytes_accessed=16 * MIB, transcendentals=0
        ),
        name=name,
    )(*heads, *weights, *came)


def whole_block(shape):
    return pl.BlockSpec(shape, lambda g: (0,) * len(shape))


def assemble_kernel(at_ref, own0, own1, other0, other1, out, sems):
    z4, z2 = at_ref[2], at_ref[3]
    up = (z4 + z2) & 3
    down = (z4 + z2 + 3) & 3
    copies = []
    for core, (src, parity, base) in enumerate(
        ((own0, z2, z4), (own1, z2, z4), (other0, 1 - z2, up), (other1, 1 - z2, down))
    ):
        for k in range(NZ4):
            copies.append(
                pltpu.make_async_copy(
                    src.at[k], out.at[core % 2, parity, (base - k) & 3], sems.at[core * NZ4 + k]
                )
            )
    for c in copies:
        c.start()
    for c in copies:
        c.wait()


def assemble_call(at, own0, own1, other0, other1):
    half = own0.shape[-1]
    return pl.pallas_call(
        assemble_kernel,
        out_shape=jax.ShapeDtypeStruct((2, NZ2, NZ4, QUARTER, half), F32),
        in_specs=[SMEM] + [ANY] * 4,
        out_specs=ANY,
        scratch_shapes=[pltpu.SemaphoreType.DMA((4 * NZ4,))],
        compiler_params=pltpu.CompilerParams(vmem_limit_bytes=56 * MIB),
        name="assemble",
    )(at, own0, own1, other0, other1)


def per_device(hidden_state, weight, targets):
    d = lax.axis_index("depth")
    z2 = lax.axis_index("z2")
    z4 = lax.axis_index("z4")
    x = lax.axis_index("x")
    y = lax.axis_index("y")
    z = z4 * NZ2 + z2
    nz = NZ4 * NZ2
    cols = weight.shape[1]
    side = cols // 2
    half = hidden_state.shape[1]
    tokens = NROW * PART
    at = jnp.stack([x, y, z4, z2]).astype(I32)

    near = lax.dynamic_slice(hidden_state, ((2 * d + z2) * PART, 0), (PART, half))
    far = swap(lax.dynamic_slice(hidden_state, ((2 * (1 - d) + z2) * PART, 0), (PART, half)), "depth")
    label = lax.dynamic_slice(targets, ((2 * d + z2) * PART,), (PART,))
    digits = jnp.stack([label % 256, (label // 256) % 256, label // 65536], axis=1).astype(BF16)
    wide = jnp.concatenate([near, far, jnp.pad(digits, ((0, 0), (0, LANES - 3)))], axis=1)
    states = lax.all_gather(wide, ROW, axis=0, tiled=True)

    from_next = shift(weight[:, :side], Z, -1)
    from_prev = shift(weight[:, side:], Z, 1)

    blocks = [weight, from_next, from_prev]
    others = [swap(b, "depth") for b in blocks]
    first = (x * NY + y) * nz
    starts = [
        (first + z) * cols,
        (first + (z + 1) % nz) * cols,
        (first + (z + nz - 1) % nz) * cols + side,
    ]
    ids = jnp.concatenate([s + jnp.arange(b.shape[1], dtype=I32) for s, b in zip(starts, blocks)])
    ids = jnp.broadcast_to(ids[None], (8, ids.shape[0]))

    logits, stats, labels = logits_call(states, ids, blocks, others)
    top, total, picked = stats[0], stats[1], stats[2]
    for axis in (ROW, "z4"):
        stats = spread(jnp.stack([top, total, picked]), axis)
        tops, totals, pickeds = stats[:, 0], stats[:, 1], stats[:, 2]
        top = tops.max(axis=0)
        total = jnp.sum(totals * jnp.exp(tops - top[None]), axis=0)
        picked = jnp.sum(pickeds, axis=0)
    lse = top + jnp.log(total)

    token_loss = lax.dynamic_slice((lse - picked).reshape(NROW, PART), (x * NY + y, 0), (1, PART)).reshape(PART)
    loss_pair = jnp.stack([token_loss, swap(token_loss, "z2")])
    loss = jnp.where(z2 == 0, loss_pair, loss_pair[::-1]).reshape(2 * PART)

    *two, slopes = product_call(
        ahead_kernel,
        [at, labels, ids, jnp.broadcast_to(lse[None], (8, tokens)), logits],
        blocks + others,
        1,
        4,
        extra_out=[jax.ShapeDtypeStruct(logits.shape, BF16)],
        extra_scratch=[pltpu.VMEM((tokens, LANES), F32)],
        name="ahead",
    )

    links = (("x", 1), ("x", -1), ("y", 1), ("y", -1))
    passed = [shift(t, ax, by) for t, (ax, by) in zip(two, links)]
    beside = product_call(beside_kernel, [at, slopes], blocks + others, 2, 4, name="beside")
    straight = [shift(t, ax, -by) for t, (ax, by) in zip(beside, links)]
    onward = product_call(onward_kernel, [at, slopes], blocks + others, 3, 8, came=passed, name="onward")

    def first_stage(sums, straight, links):
        last = [shift(after(t, s), ax, by) for t, s, (ax, by) in zip(sums[:2], reversed(straight), links)]
        held = lax.optimization_barrier([o + s for o, s in zip(sums[2:], straight)])
        return jnp.concatenate([h + l for h, l in zip(held, last)], axis=1)

    near_x = first_stage(onward[0:4], straight[0:2], links[:2]).reshape(NY, PART, half)
    far_y = first_stage(onward[4:8], straight[2:4], links[2:]).reshape(NX, PART, half)

    def ring_sum(parts, axis):
        terms = [parts[0]] + [shift(p, axis, s) for s, p in enumerate(parts) if s]
        return terms[0] + terms[1] + terms[2] + terms[3]

    near_grad = ring_sum([lax.dynamic_index_in_dim(near_x, (y + s) % NY, 0, False) for s in range(NY)], "y")
    far_grad = ring_sum([lax.dynamic_index_in_dim(far_y, (x + s) % NX, 0, False) for s in range(NX)], "x")
    crossed = swap(far_grad, "depth")
    pair = jnp.stack([near_grad, crossed])
    pair = jnp.where(d == 0, pair, pair[::-1]).reshape(2, NZ4, QUARTER, half)
    done = ring_sum([lax.dynamic_index_in_dim(pair, (z4 + s) % NZ4, 1, False) for s in range(NZ4)], "z4")
    copies = ring_copies(done, "z4", NZ4)
    own0 = jnp.stack([c[0] for c in copies])
    own1 = jnp.stack([c[1] for c in copies])
    other0 = shift(own0, Z, -1)
    other1 = shift(own1, Z, 1)
    grad = assemble_call(at, own0, own1, other0, other1).reshape(4 * PART, half)
    return loss, grad


def solution(mesh):
    fine = Mesh(mesh.devices.reshape(NX, NY, NZ4, NZ2, 2), ("x", "y", "z4", "z2", "depth"))
    return jax.shard_map(
        per_device,
        mesh=fine,
        in_specs=(P(ROW, "depth"), P("depth", ROW + Z), P(ROW)),
        out_specs=(P(ROW + ("depth",)), P(ROW, "depth")),
        check_vma=False,
    )
```

```python
import functools

import jax
import jax.numpy as jnp
from jax import lax
from jax.experimental import pallas as pl
from jax.experimental.pallas import tpu as pltpu
from jax.sharding import Mesh, PartitionSpec as P

F32 = jnp.float32
BF16 = jnp.bfloat16
I32 = jnp.int32
ROW = ("x", "y")
Z = ("z4", "z2")
NX, NY, NZ4, NZ2 = 4, 4, 4, 2
NROW = NX * NY
PART = 32
QUARTER = PART // NZ4
LANES = 128
CHUNK = 32
WIDE = 768
TILE = 512
MIB = 1024 * 1024
ANY = pl.BlockSpec(memory_space=pl.ANY)
SMEM = pl.BlockSpec(memory_space=pltpu.SMEM)
VMEM = pl.BlockSpec(memory_space=pltpu.VMEM)


def shift(value, axis, by):
    n = lax.axis_size(axis)
    return lax.ppermute(value, axis, [(i, (i + by) % n) for i in range(n)])


def swap(value, axis):
    return lax.ppermute(value, axis, [(0, 1), (1, 0)])


def cross_shift(value, axis, by):
    n = lax.axis_size(axis)
    pairs = [(2 * i + c, 2 * ((i + by) % n) + 1 - c) for i in range(n) for c in range(2)]
    return lax.ppermute(value, (axis, "depth"), pairs)


def after(value, earlier):
    return lax.optimization_barrier((value, earlier))[0]


def spread(value, axis):
    n = lax.axis_size(axis)
    return lax.all_to_all(jnp.broadcast_to(value[None], (n,) + value.shape), axis, 0, 0, tiled=True)


def ring_copies(value, axis, n):
    return [value] + [shift(value, axis, s) for s in range(1, n)]


def column(row_ref, tokens):
    return jnp.transpose(jnp.broadcast_to(row_ref[0:1, :], (LANES, tokens)))


def logits_kernel(at_ref, states, ids_ref, *refs):
    near, far, far_blocks = refs[0:3], refs[3:6], refs[6 : 6 + NX]
    x, y = at_ref[0], at_ref[1]
    logits_ref, stats_ref, lab, xn, xf, wn, wf, digits, tops, sums, picks, sems = refs[6 + NX :]
    tokens, cols = logits_ref.shape
    half, own = near[0].shape
    side = near[1].shape[1]
    count = [0]

    def copy(src, dst):
        count[0] += 1
        return pltpu.make_async_copy(src, dst, sems.at[count[0] - 1])

    label = copy(states.at[:, pl.ds(half, LANES)], digits)
    sides = [pl.ds(own, side), pl.ds(own + side, side)]
    far_states = [
        copy(
            far_blocks[i].at[j],
            xf.at[pl.ds(pl.multiple_of((((x - i) & 3) * NY + ((y - j) & 3)) * PART, PART), PART)],
        )
        for i in range(NX)
        for j in range(NY)
    ]
    needs = [
        [copy(states.at[:, pl.ds(0, half)], xn), copy(near[0], wn.at[:, pl.ds(0, own)])],
        far_states + [copy(far[0], wf.at[:, pl.ds(0, own)])],
        [copy(near[k + 1], wn.at[:, sides[k]]) for k in range(2)],
        [copy(far[k + 1], wf.at[:, sides[k]]) for k in range(2)],
    ]

    def start(t):
        for c in needs[t] if t < len(needs) else []:
            c.start()

    label.start()
    start(0)
    start(1)
    label.wait()
    v = digits[...].astype(F32)
    code = v[:, 0:1] + 256.0 * v[:, 1:2] + 65536.0 * v[:, 2:3]
    lab[...] = jnp.broadcast_to(code, (tokens, LANES)).astype(I32)

    for t in range(cols // WIDE):
        c = pl.ds(t * WIDE, WIDE)
        for k in (2 * t, 2 * t + 1):
            for copied in needs[k]:
                copied.wait()
            start(k + 2)
            if k % 2 == 0:
                logits_ref[:, c] = jnp.dot(xn[...], wn[:, c], preferred_element_type=F32)
        v = logits_ref[:, c] + jnp.dot(xf[...], wf[:, c], preferred_element_type=F32)
        logits_ref[:, c] = v
        parts = [v[:, k * LANES : (k + 1) * LANES] for k in range(WIDE // LANES)]
        top = functools.reduce(jnp.maximum, parts)
        if t:
            top = jnp.maximum(tops[...], top)
        total = sum(jnp.exp(p - top) for p in parts)
        picked = None
        for k, p in enumerate(parts):
            hit = ids_ref[0:1, pl.ds(t * WIDE + k * LANES, LANES)] == lab[...]
            mine = jnp.where(hit, p, 0.0)
            picked = mine if picked is None else picked + mine
        sums[...] = total + sums[...] * jnp.exp(tops[...] - top) if t else total
        picks[...] = picks[...] + picked if t else picked
        tops[...] = top

    top = jnp.max(tops[...], axis=1, keepdims=True)
    total = jnp.sum(sums[...] * jnp.exp(tops[...] - top), axis=1, keepdims=True)
    picked = jnp.sum(picks[...], axis=1, keepdims=True)
    lane = lax.broadcasted_iota(I32, (tokens, LANES), 1)
    packed = jnp.where(lane == 0, top, jnp.where(lane == 1, total, picked))
    stats_ref[...] = jnp.transpose(packed)[0:8, :]


def logits_call(at, states, far_blocks, ids, near, far):
    half = near[0].shape[0]
    tokens = states.shape[0]
    cols = ids.shape[1]
    return pl.pallas_call(
        logits_kernel,
        out_shape=(
            pltpu.HBM((tokens, cols), F32),
            jax.ShapeDtypeStruct((8, tokens), F32),
            jax.ShapeDtypeStruct((tokens, LANES), I32),
        ),
        in_specs=[SMEM, ANY, VMEM] + [ANY] * (6 + NX),
        out_specs=(VMEM, VMEM, VMEM),
        scratch_shapes=[
            pltpu.VMEM((tokens, half), BF16),
            pltpu.VMEM((tokens, half), BF16),
            pltpu.VMEM((half, cols), BF16),
            pltpu.VMEM((half, cols), BF16),
            pltpu.VMEM((tokens, LANES), BF16),
            pltpu.VMEM((tokens, LANES), F32),
            pltpu.VMEM((tokens, LANES), F32),
            pltpu.VMEM((tokens, LANES), F32),
            pltpu.SemaphoreType.DMA((32,)),
        ],
        compiler_params=pltpu.CompilerParams(vmem_limit_bytes=28 * MIB),
        cost_estimate=pl.CostEstimate(
            flops=4 * tokens * half * cols, bytes_accessed=20 * MIB, transcendentals=tokens * cols
        ),
        name="logits",
    )(at, states, ids, *near, *far, *far_blocks)


def contract(slopes_ref, w0, w1, w2, first=0, last=None):
    own, side = w0.shape[1], w1.shape[1]
    slopes = slopes_ref[first:last, :]

    def nt(a, b):
        return lax.dot_general(a, b, (((1,), (1,)), ((), ())), preferred_element_type=F32)

    return (
        nt(slopes[:, 0:own], w0[...])
        + nt(slopes[:, own : own + side], w1[...])
        + nt(slopes[:, own + side :], w2[...])
    )


def pick_rows(at_ref, slopes_ref, near_rows, far_rows, steps):
    x, y = at_ref[0], at_ref[1]
    span = NY * PART
    for k, s in enumerate(steps):
        start = pl.multiple_of(((x + s) & 3) * span, span)
        near_rows[pl.ds(k * span, span), :] = slopes_ref[pl.ds(start, span), :]
        for a in range(NX):
            start = pl.multiple_of((a * NY + ((y + s) & 3)) * PART, PART)
            far_rows[pl.ds(k * span + a * PART, PART), :] = slopes_ref[pl.ds(start, PART), :]


def ahead_kernel(at_ref, lab, ids_ref, lse_ref, logits_ref, *refs):
    near_w, far_w, near_out, far_out = refs[0:3], refs[3:6], refs[6:8], refs[8:10]
    slopes_ref, lse, near_rows, far_rows = refs[10:]
    tokens = logits_ref.shape[0]
    step = pl.program_id(0)

    @pl.when(step == 0)
    def _():
        lse[...] = column(lse_ref, tokens)

        def chunk(k, _):
            r = pl.ds(pl.multiple_of(k * CHUNK, CHUNK), CHUNK)
            hit = ids_ref[0:1, :] == lab[r, 0:1]
            p = jnp.exp(logits_ref[r, :] - lse[r, 0:1])
            slopes_ref[r, :] = (p - jnp.where(hit, 1.0, 0.0)).astype(BF16)
            return 0

        lax.fori_loop(0, tokens // CHUNK, chunk, 0)
        pick_rows(at_ref, slopes_ref, near_rows, far_rows, (2,))

    near_v, far_v = contract(near_rows, *near_w), contract(far_rows, *far_w)
    for side in range(2):

        @pl.when(step // 2 == side)
        def _(side=side):
            near_out[side][...] = near_v
            far_out[side][...] = far_v


def beside_kernel(at_ref, slopes_ref, *refs):
    near_w, far_w, near_out, far_out = refs[0:3], refs[3:6], refs[6:8], refs[8:10]
    near_rows, far_rows = refs[10:]
    step = pl.program_id(0)
    span = NY * PART

    @pl.when(step == 0)
    def _():
        pick_rows(at_ref, slopes_ref, near_rows, far_rows, (3, 1))

    for side in range(2):

        @pl.when(step // 2 == side)
        def _(side=side):
            at = (side * span, (side + 1) * span)
            near_out[side][...] = contract(near_rows, *near_w, *at)
            far_out[side][...] = contract(far_rows, *far_w, *at)


def onward_kernel(at_ref, slopes_ref, *refs):
    near_w, far_w, near_in, far_in = refs[0:3], refs[3:6], refs[6:8], refs[8:10]
    near_out, far_out = refs[10:14], refs[14:18]
    near_rows, far_rows = refs[18:]
    step = pl.program_id(0)
    span = NY * PART

    @pl.when(step == 0)
    def _():
        pick_rows(at_ref, slopes_ref, near_rows, far_rows, (1, 0, 3))

    for side in range(2):

        @pl.when(step // 2 == side)
        def _(side=side):
            for rows, w, came, out in ((near_rows, near_w, near_in, near_out), (far_rows, far_w, far_in, far_out)):
                v = contract(rows, *w, side * span, (side + 2) * span)
                sent = v[side * span : (side + 1) * span]
                out[side][...] = sent + came[side][...]
                out[2 + side][...] = v[(1 - side) * span : (2 - side) * span]


def product_call(
    kernel, heads, weights, blocks, outs, came=(), extra_out=(), extra_scratch=(), name=None, kind=jax.ShapeDtypeStruct
):
    half = weights[0].shape[0]
    cols = sum(w.shape[1] for w in weights) // 2
    span = NY * PART
    part = kind((span, half // 2), F32)
    left = pl.BlockSpec((span, TILE), lambda g: (0, jnp.minimum(g, 1)))
    right = pl.BlockSpec((span, TILE), lambda g: (0, jnp.maximum(g - 2, 0)))
    rows = pltpu.VMEM((blocks * span, cols), BF16)
    return pl.pallas_call(
        kernel,
        grid=(half // TILE,),
        out_shape=tuple([part] * outs + list(extra_out)),
        in_specs=[SMEM]
        + [whole_block(h.shape) for h in heads[1:]]
        + [pl.BlockSpec((TILE, w.shape[1]), lambda g: (g, 0)) for w in weights]
        + [left, right] * (len(came) // 2),
        out_specs=tuple([left, right] * (outs // 2) + [whole_block(e.shape) for e in extra_out]),
        scratch_shapes=list(extra_scratch) + [rows, rows],
        compiler_params=pltpu.CompilerParams(vmem_limit_bytes=24 * MIB),
        cost_estimate=pl.CostEstimate(
            flops=outs * span * half * cols, bytes_accessed=16 * MIB, transcendentals=0
        ),
        name=name,
    )(*heads, *weights, *came)


def whole_block(shape):
    return pl.BlockSpec(shape, lambda g: (0,) * len(shape))


def assemble_kernel(at_ref, own0, own1, other0, other1, out, sems):
    z4, z2 = at_ref[2], at_ref[3]
    up = (z4 + z2) & 3
    down = (z4 + z2 + 3) & 3
    copies = []
    for core, (src, parity, base) in enumerate(
        ((own0, z2, z4), (own1, z2, z4), (other0, 1 - z2, up), (other1, 1 - z2, down))
    ):
        for k in range(NZ4):
            copies.append(
                pltpu.make_async_copy(
                    src.at[k], out.at[core % 2, parity, (base - k) & 3], sems.at[core * NZ4 + k]
                )
            )
    for c in copies:
        c.start()
    for c in copies:
        c.wait()


def assemble_call(at, own0, own1, other0, other1):
    half = own0.shape[-1]
    return pl.pallas_call(
        assemble_kernel,
        out_shape=jax.ShapeDtypeStruct((2, NZ2, NZ4, QUARTER, half), F32),
        in_specs=[SMEM] + [ANY] * 4,
        out_specs=ANY,
        scratch_shapes=[pltpu.SemaphoreType.DMA((4 * NZ4,))],
        compiler_params=pltpu.CompilerParams(vmem_limit_bytes=24 * MIB),
        name="assemble",
    )(at, own0, own1, other0, other1)


def per_device(hidden_state, weight, targets):
    d = lax.axis_index("depth")
    z2 = lax.axis_index("z2")
    z4 = lax.axis_index("z4")
    x = lax.axis_index("x")
    y = lax.axis_index("y")
    z = z4 * NZ2 + z2
    nz = NZ4 * NZ2
    cols = weight.shape[1]
    side = cols // 2
    half = hidden_state.shape[1]
    tokens = NROW * PART
    at = jnp.stack([x, y, z4, z2]).astype(I32)

    near = lax.dynamic_slice(hidden_state, ((2 * d + z2) * PART, 0), (PART, half))
    crossing = lax.dynamic_slice(hidden_state, ((2 * (1 - d) + z2) * PART, 0), (PART, half))
    label = lax.dynamic_slice(targets, ((2 * d + z2) * PART,), (PART,))
    digits = jnp.stack([label % 256, (label // 256) % 256, label // 65536], axis=1).astype(BF16)
    wide = jnp.concatenate([near, jnp.pad(digits, ((0, 0), (0, LANES - 3)))], axis=1)
    states = lax.all_gather(wide, ROW, axis=0, tiled=True)

    from_next = shift(weight[:, :side], Z, -1)
    from_prev = shift(weight[:, side:], Z, 1)

    far_line = jnp.stack([cross_shift(crossing, "y", s) for s in range(NY)])
    far_blocks = [far_line] + [shift(far_line, "x", s) for s in range(1, NX)]

    blocks = [weight, from_next, from_prev]
    others = [swap(after(b, far_blocks[1:]), "depth") for b in blocks]
    first = (x * NY + y) * nz
    starts = [
        (first + z) * cols,
        (first + (z + 1) % nz) * cols,
        (first + (z + nz - 1) % nz) * cols + side,
    ]
    ids = jnp.concatenate([s + jnp.arange(b.shape[1], dtype=I32) for s, b in zip(starts, blocks)])
    ids = jnp.broadcast_to(ids[None], (8, ids.shape[0]))

    logits, stats, labels = logits_call(at, states, far_blocks, ids, blocks, others)
    top, total, picked = stats[0], stats[1], stats[2]
    for axis in (ROW, "z4"):
        stats = spread(jnp.stack([top, total, picked]), axis)
        tops, totals, pickeds = stats[:, 0], stats[:, 1], stats[:, 2]
        top = tops.max(axis=0)
        total = jnp.sum(totals * jnp.exp(tops - top[None]), axis=0)
        picked = jnp.sum(pickeds, axis=0)
    lse = top + jnp.log(total)

    token_loss = lax.dynamic_slice((lse - picked).reshape(NROW, PART), (x * NY + y, 0), (1, PART)).reshape(PART)
    loss_pair = jnp.stack([token_loss, swap(token_loss, "z2")])
    loss = jnp.where(z2 == 0, loss_pair, loss_pair[::-1]).reshape(2 * PART)

    *two, slopes = product_call(
        ahead_kernel,
        [at, labels, ids, jnp.broadcast_to(lse[None], (8, tokens)), logits],
        blocks + others,
        1,
        4,
        extra_out=[jax.ShapeDtypeStruct(logits.shape, BF16)],
        extra_scratch=[pltpu.VMEM((tokens, LANES), F32)],
        name="ahead",
    )

    links = (("x", 1), ("x", -1), ("y", 1), ("y", -1))
    passed = [shift(t, ax, by) for t, (ax, by) in zip(two, links)]
    beside = product_call(beside_kernel, [at, slopes], blocks + others, 2, 4, name="beside")
    straight = [shift(t, ax, -by) for t, (ax, by) in zip(beside, links)]
    onward = product_call(onward_kernel, [at, slopes], blocks + others, 3, 8, came=passed, name="onward", kind=pltpu.HBM)

    def first_stage(sums, straight, links):
        last = [shift(after(t, s), ax, by) for t, s, (ax, by) in zip(sums[:2], reversed(straight), links)]
        held = lax.optimization_barrier([o + s for o, s in zip(sums[2:], straight)])
        return jnp.concatenate([h + l for h, l in zip(held, last)], axis=1)

    near_x = first_stage(onward[0:4], straight[0:2], links[:2]).reshape(NY, PART, half)
    far_y = first_stage(onward[4:8], straight[2:4], links[2:]).reshape(NX, PART, half)

    def ring_sum(parts, axis):
        terms = [parts[0]] + [shift(p, axis, s) for s, p in enumerate(parts) if s]
        return terms[0] + terms[1] + terms[2] + terms[3]

    near_grad = ring_sum([lax.dynamic_index_in_dim(near_x, (y + s) % NY, 0, False) for s in range(NY)], "y")
    far_grad = ring_sum([lax.dynamic_index_in_dim(far_y, (x + s) % NX, 0, False) for s in range(NX)], "x")
    crossed = swap(far_grad, "depth")
    pair = jnp.stack([near_grad, crossed])
    pair = jnp.where(d == 0, pair, pair[::-1]).reshape(2, NZ4, QUARTER, half)
    done = ring_sum([lax.dynamic_index_in_dim(pair, (z4 + s) % NZ4, 1, False) for s in range(NZ4)], "z4")
    copies = ring_copies(done, "z4", NZ4)
    own0 = jnp.stack([c[0] for c in copies])
    own1 = jnp.stack([c[1] for c in copies])
    other0 = shift(own0, Z, -1)
    other1 = shift(own1, Z, 1)
    grad = assemble_call(at, own0, own1, other0, other1).reshape(4 * PART, half)
    return loss, grad


def solution(mesh):
    fine = Mesh(mesh.devices.reshape(NX, NY, NZ4, NZ2, 2), ("x", "y", "z4", "z2", "depth"))
    return jax.shard_map(
        per_device,
        mesh=fine,
        in_specs=(P(ROW, "depth"), P("depth", ROW + Z), P(ROW)),
        out_specs=(P(ROW + ("depth",)), P(ROW, "depth")),
        check_vma=False,
    )
```

```python
import functools

import jax
import jax.numpy as jnp
from jax import lax
from jax.experimental import pallas as pl
from jax.experimental.pallas import tpu as pltpu
from jax.sharding import Mesh, PartitionSpec as P

F32 = jnp.float32
BF16 = jnp.bfloat16
I32 = jnp.int32
ROW = ("x", "y")
Z = ("z4", "z2")
NX, NY, NZ4, NZ2 = 4, 4, 4, 2
NROW = NX * NY
PART = 32
QUARTER = PART // NZ4
LANES = 128
CHUNK = 32
WIDE = 768
TILE = 512
MIB = 1024 * 1024
ANY = pl.BlockSpec(memory_space=pl.ANY)
SMEM = pl.BlockSpec(memory_space=pltpu.SMEM)
VMEM = pl.BlockSpec(memory_space=pltpu.VMEM)


def shift(value, axis, by):
    n = lax.axis_size(axis)
    return lax.ppermute(value, axis, [(i, (i + by) % n) for i in range(n)])


def swap(value, axis):
    return lax.ppermute(value, axis, [(0, 1), (1, 0)])


def after(value, earlier):
    return lax.optimization_barrier((value, earlier))[0]


def spread(value, axis):
    n = lax.axis_size(axis)
    return lax.all_to_all(jnp.broadcast_to(value[None], (n,) + value.shape), axis, 0, 0, tiled=True)


def ring_copies(value, axis, n):
    return [value] + [shift(value, axis, s) for s in range(1, n)]


def column(row_ref, tokens):
    return jnp.transpose(jnp.broadcast_to(row_ref[0:1, :], (LANES, tokens)))


def logits_kernel(states, ids_ref, *refs):
    near, far = refs[0:3], refs[3:6]
    logits_ref, stats_ref, lab, xn, xf, wn, wf, digits, tops, sums, picks, sems = refs[6:]
    tokens, cols = logits_ref.shape
    half, own = near[0].shape
    side = near[1].shape[1]
    count = [0]

    def copy(src, dst):
        count[0] += 1
        return pltpu.make_async_copy(src, dst, sems.at[count[0] - 1])

    label = copy(states.at[:, pl.ds(2 * half, LANES)], digits)
    sides = [pl.ds(own, side), pl.ds(own + side, side)]
    needs = [
        [copy(states.at[:, pl.ds(0, half)], xn), copy(near[0], wn.at[:, pl.ds(0, own)])],
        [copy(states.at[:, pl.ds(half, half)], xf), copy(far[0], wf.at[:, pl.ds(0, own)])],
        [copy(near[k + 1], wn.at[:, sides[k]]) for k in range(2)],
        [copy(far[k + 1], wf.at[:, sides[k]]) for k in range(2)],
    ]

    def start(t):
        for c in needs[t] if t < len(needs) else []:
            c.start()

    label.start()
    start(0)
    start(1)
    label.wait()
    v = digits[...].astype(F32)
    code = v[:, 0:1] + 256.0 * v[:, 1:2] + 65536.0 * v[:, 2:3]
    lab[...] = jnp.broadcast_to(code, (tokens, LANES)).astype(I32)

    for t in range(cols // WIDE):
        c = pl.ds(t * WIDE, WIDE)
        for k in (2 * t, 2 * t + 1):
            for copied in needs[k]:
                copied.wait()
            start(k + 2)
            if k % 2 == 0:
                logits_ref[:, c] = jnp.dot(xn[...], wn[:, c], preferred_element_type=F32)
        v = logits_ref[:, c] + jnp.dot(xf[...], wf[:, c], preferred_element_type=F32)
        logits_ref[:, c] = v
        parts = [v[:, k * LANES : (k + 1) * LANES] for k in range(WIDE // LANES)]
        top = functools.reduce(jnp.maximum, parts)
        if t:
            top = jnp.maximum(tops[...], top)
        total = sum(jnp.exp(p - top) for p in parts)
        picked = None
        for k, p in enumerate(parts):
            hit = ids_ref[0:1, pl.ds(t * WIDE + k * LANES, LANES)] == lab[...]
            mine = jnp.where(hit, p, 0.0)
            picked = mine if picked is None else picked + mine
        sums[...] = total + sums[...] * jnp.exp(tops[...] - top) if t else total
        picks[...] = picks[...] + picked if t else picked
        tops[...] = top

    top = jnp.max(tops[...], axis=1, keepdims=True)
    total = jnp.sum(sums[...] * jnp.exp(tops[...] - top), axis=1, keepdims=True)
    picked = jnp.sum(picks[...], axis=1, keepdims=True)
    lane = lax.broadcasted_iota(I32, (tokens, LANES), 1)
    packed = jnp.where(lane == 0, top, jnp.where(lane == 1, total, picked))
    stats_ref[...] = jnp.transpose(packed)[0:8, :]


def logits_call(states, ids, near, far):
    half = near[0].shape[0]
    tokens = states.shape[0]
    cols = ids.shape[1]
    return pl.pallas_call(
        logits_kernel,
        out_shape=(
            pltpu.HBM((tokens, cols), F32),
            jax.ShapeDtypeStruct((8, tokens), F32),
            jax.ShapeDtypeStruct((tokens, LANES), I32),
        ),
        in_specs=[ANY, VMEM] + [ANY] * 6,
        out_specs=(VMEM, VMEM, VMEM),
        scratch_shapes=[
            pltpu.VMEM((tokens, half), BF16),
            pltpu.VMEM((tokens, half), BF16),
            pltpu.VMEM((half, cols), BF16),
            pltpu.VMEM((half, cols), BF16),
            pltpu.VMEM((tokens, LANES), BF16),
            pltpu.VMEM((tokens, LANES), F32),
            pltpu.VMEM((tokens, LANES), F32),
            pltpu.VMEM((tokens, LANES), F32),
            pltpu.SemaphoreType.DMA((32,)),
        ],
        compiler_params=pltpu.CompilerParams(vmem_limit_bytes=28 * MIB),
        cost_estimate=pl.CostEstimate(
            flops=4 * tokens * half * cols, bytes_accessed=20 * MIB, transcendentals=tokens * cols
        ),
        name="logits",
    )(states, ids, *near, *far)


def contract(slopes_ref, w0, w1, w2, first=0, last=None):
    own, side = w0.shape[1], w1.shape[1]
    slopes = slopes_ref[first:last, :]

    def nt(a, b):
        return lax.dot_general(a, b, (((1,), (1,)), ((), ())), preferred_element_type=F32)

    return (
        nt(slopes[:, 0:own], w0[...])
        + nt(slopes[:, own : own + side], w1[...])
        + nt(slopes[:, own + side :], w2[...])
    )


def pick_rows(at_ref, slopes_ref, near_rows, far_rows, steps):
    x, y = at_ref[0], at_ref[1]
    span = NY * PART
    for k, s in enumerate(steps):
        start = pl.multiple_of(((x + s) & 3) * span, span)
        near_rows[pl.ds(k * span, span), :] = slopes_ref[pl.ds(start, span), :]
        for a in range(NX):
            start = pl.multiple_of((a * NY + ((y + s) & 3)) * PART, PART)
            far_rows[pl.ds(k * span + a * PART, PART), :] = slopes_ref[pl.ds(start, PART), :]


def ahead_kernel(at_ref, lab, ids_ref, lse_ref, logits_ref, *refs):
    near_w, far_w, near_out, far_out = refs[0:3], refs[3:6], refs[6:8], refs[8:10]
    slopes_ref, lse, near_rows, far_rows = refs[10:]
    tokens = logits_ref.shape[0]
    step = pl.program_id(0)

    @pl.when(step == 0)
    def _():
        lse[...] = column(lse_ref, tokens)

        def chunk(k, _):
            r = pl.ds(pl.multiple_of(k * CHUNK, CHUNK), CHUNK)
            hit = ids_ref[0:1, :] == lab[r, 0:1]
            p = jnp.exp(logits_ref[r, :] - lse[r, 0:1])
            slopes_ref[r, :] = (p - jnp.where(hit, 1.0, 0.0)).astype(BF16)
            return 0

        lax.fori_loop(0, tokens // CHUNK, chunk, 0)
        pick_rows(at_ref, slopes_ref, near_rows, far_rows, (2,))

    near_v, far_v = contract(near_rows, *near_w), contract(far_rows, *far_w)
    for side in range(2):

        @pl.when(step // 2 == side)
        def _(side=side):
            near_out[side][...] = near_v
            far_out[side][...] = far_v


def beside_kernel(at_ref, slopes_ref, *refs):
    near_w, far_w, near_out, far_out = refs[0:3], refs[3:6], refs[6:8], refs[8:10]
    near_rows, far_rows = refs[10:]
    step = pl.program_id(0)
    span = NY * PART

    @pl.when(step == 0)
    def _():
        pick_rows(at_ref, slopes_ref, near_rows, far_rows, (3, 1))

    for side in range(2):

        @pl.when(step // 2 == side)
        def _(side=side):
            at = (side * span, (side + 1) * span)
            near_out[side][...] = contract(near_rows, *near_w, *at)
            far_out[side][...] = contract(far_rows, *far_w, *at)


def onward_kernel(at_ref, slopes_ref, *refs):
    near_w, far_w, near_in, far_in = refs[0:3], refs[3:6], refs[6:8], refs[8:10]
    near_out, far_out = refs[10:14], refs[14:18]
    near_rows, far_rows = refs[18:]
    step = pl.program_id(0)
    span = NY * PART

    @pl.when(step == 0)
    def _():
        pick_rows(at_ref, slopes_ref, near_rows, far_rows, (1, 0, 3))

    for side in range(2):

        @pl.when(step // 2 == side)
        def _(side=side):
            for rows, w, came, out in ((near_rows, near_w, near_in, near_out), (far_rows, far_w, far_in, far_out)):
                v = contract(rows, *w, side * span, (side + 2) * span)
                sent = v[side * span : (side + 1) * span]
                out[side][...] = sent + came[side][...]
                out[2 + side][...] = v[(1 - side) * span : (2 - side) * span]


def product_call(
    kernel, heads, weights, blocks, outs, came=(), extra_out=(), extra_scratch=(), name=None, kind=jax.ShapeDtypeStruct
):
    half = weights[0].shape[0]
    cols = sum(w.shape[1] for w in weights) // 2
    span = NY * PART
    part = kind((span, half // 2), F32)
    left = pl.BlockSpec((span, TILE), lambda g: (0, jnp.minimum(g, 1)))
    right = pl.BlockSpec((span, TILE), lambda g: (0, jnp.maximum(g - 2, 0)))
    rows = pltpu.VMEM((blocks * span, cols), BF16)
    return pl.pallas_call(
        kernel,
        grid=(half // TILE,),
        out_shape=tuple([part] * outs + list(extra_out)),
        in_specs=[SMEM]
        + [whole_block(h.shape) for h in heads[1:]]
        + [pl.BlockSpec((TILE, w.shape[1]), lambda g: (g, 0)) for w in weights]
        + [left, right] * (len(came) // 2),
        out_specs=tuple([left, right] * (outs // 2) + [whole_block(e.shape) for e in extra_out]),
        scratch_shapes=list(extra_scratch) + [rows, rows],
        compiler_params=pltpu.CompilerParams(vmem_limit_bytes=24 * MIB),
        cost_estimate=pl.CostEstimate(
            flops=outs * span * half * cols, bytes_accessed=16 * MIB, transcendentals=0
        ),
        name=name,
    )(*heads, *weights, *came)


def whole_block(shape):
    return pl.BlockSpec(shape, lambda g: (0,) * len(shape))


def assemble_kernel(at_ref, own0, own1, other0, other1, out, sems):
    z4, z2 = at_ref[2], at_ref[3]
    up = (z4 + z2) & 3
    down = (z4 + z2 + 3) & 3
    copies = []
    for core, (src, parity, base) in enumerate(
        ((own0, z2, z4), (own1, z2, z4), (other0, 1 - z2, up), (other1, 1 - z2, down))
    ):
        for k in range(NZ4):
            copies.append(
                pltpu.make_async_copy(
                    src.at[k], out.at[core % 2, parity, (base - k) & 3], sems.at[core * NZ4 + k]
                )
            )
    for c in copies:
        c.start()
    for c in copies:
        c.wait()


def assemble_call(at, own0, own1, other0, other1):
    half = own0.shape[-1]
    return pl.pallas_call(
        assemble_kernel,
        out_shape=jax.ShapeDtypeStruct((2, NZ2, NZ4, QUARTER, half), F32),
        in_specs=[SMEM] + [ANY] * 4,
        out_specs=ANY,
        scratch_shapes=[pltpu.SemaphoreType.DMA((4 * NZ4,))],
        compiler_params=pltpu.CompilerParams(vmem_limit_bytes=24 * MIB),
        name="assemble",
    )(at, own0, own1, other0, other1)


def per_device(hidden_state, weight, targets):
    d = lax.axis_index("depth")
    z2 = lax.axis_index("z2")
    z4 = lax.axis_index("z4")
    x = lax.axis_index("x")
    y = lax.axis_index("y")
    z = z4 * NZ2 + z2
    nz = NZ4 * NZ2
    cols = weight.shape[1]
    side = cols // 2
    half = hidden_state.shape[1]
    tokens = NROW * PART
    at = jnp.stack([x, y, z4, z2]).astype(I32)

    near = lax.dynamic_slice(hidden_state, ((2 * d + z2) * PART, 0), (PART, half))
    far = swap(lax.dynamic_slice(hidden_state, ((2 * (1 - d) + z2) * PART, 0), (PART, half)), "depth")
    label = lax.dynamic_slice(targets, ((2 * d + z2) * PART,), (PART,))
    digits = jnp.stack([label % 256, (label // 256) % 256, label // 65536], axis=1).astype(BF16)
    wide = jnp.concatenate([near, far, jnp.pad(digits, ((0, 0), (0, LANES - 3)))], axis=1)
    states = lax.all_gather(wide, ROW, axis=0, tiled=True)

    from_next = shift(weight[:, :side], Z, -1)
    from_prev = shift(weight[:, side:], Z, 1)

    blocks = [weight, from_next, from_prev]
    others = [swap(b, "depth") for b in blocks]
    first = (x * NY + y) * nz
    starts = [
        (first + z) * cols,
        (first + (z + 1) % nz) * cols,
        (first + (z + nz - 1) % nz) * cols + side,
    ]
    ids = jnp.concatenate([s + jnp.arange(b.shape[1], dtype=I32) for s, b in zip(starts, blocks)])
    ids = jnp.broadcast_to(ids[None], (8, ids.shape[0]))

    logits, stats, labels = logits_call(states, ids, blocks, others)
    top, total, picked = stats[0], stats[1], stats[2]
    for axis in (ROW, "z4"):
        stats = spread(jnp.stack([top, total, picked]), axis)
        tops, totals, pickeds = stats[:, 0], stats[:, 1], stats[:, 2]
        top = tops.max(axis=0)
        total = jnp.sum(totals * jnp.exp(tops - top[None]), axis=0)
        picked = jnp.sum(pickeds, axis=0)
    lse = top + jnp.log(total)

    token_loss = lax.dynamic_slice((lse - picked).reshape(NROW, PART), (x * NY + y, 0), (1, PART)).reshape(PART)
    loss_pair = jnp.stack([token_loss, swap(token_loss, "z2")])
    loss = jnp.where(z2 == 0, loss_pair, loss_pair[::-1]).reshape(2 * PART)

    *two, slopes = product_call(
        ahead_kernel,
        [at, labels, ids, jnp.broadcast_to(lse[None], (8, tokens)), logits],
        blocks + others,
        1,
        4,
        extra_out=[jax.ShapeDtypeStruct(logits.shape, BF16)],
        extra_scratch=[pltpu.VMEM((tokens, LANES), F32)],
        name="ahead",
    )

    links = (("x", 1), ("x", -1), ("y", 1), ("y", -1))
    passed = [shift(t, ax, by) for t, (ax, by) in zip(two, links)]
    beside = product_call(beside_kernel, [at, slopes], blocks + others, 2, 4, name="beside")
    straight = [shift(t, ax, -by) for t, (ax, by) in zip(beside, links)]
    onward = product_call(onward_kernel, [at, slopes], blocks + others, 3, 8, came=passed, name="onward", kind=pltpu.HBM)

    def first_stage(sums, straight, links):
        last = [shift(after(t, s), ax, by) for t, s, (ax, by) in zip(sums[:2], reversed(straight), links)]
        held = lax.optimization_barrier([o + s for o, s in zip(sums[2:], straight)])
        return jnp.concatenate([h + l for h, l in zip(held, last)], axis=1)

    near_x = first_stage(onward[0:4], straight[0:2], links[:2]).reshape(NY, PART, half)
    far_y = first_stage(onward[4:8], straight[2:4], links[2:]).reshape(NX, PART, half)

    def ring_sum(parts, axis):
        terms = [parts[0]] + [shift(p, axis, s) for s, p in enumerate(parts) if s]
        return terms[0] + terms[1] + terms[2] + terms[3]

    near_grad = ring_sum([lax.dynamic_index_in_dim(near_x, (y + s) % NY, 0, False) for s in range(NY)], "y")
    far_grad = ring_sum([lax.dynamic_index_in_dim(far_y, (x + s) % NX, 0, False) for s in range(NX)], "x")
    crossed = swap(far_grad, "depth")
    pair = jnp.stack([near_grad, crossed])
    pair = jnp.where(d == 0, pair, pair[::-1]).reshape(2, NZ4, QUARTER, half)
    done = ring_sum([lax.dynamic_index_in_dim(pair, (z4 + s) % NZ4, 1, False) for s in range(NZ4)], "z4")
    copies = ring_copies(done, "z4", NZ4)
    own0 = jnp.stack([c[0] for c in copies])
    own1 = jnp.stack([c[1] for c in copies])
    other0 = shift(own0, Z, -1)
    other1 = shift(own1, Z, 1)
    grad = assemble_call(at, own0, own1, other0, other1).reshape(4 * PART, half)
    return loss, grad


def solution(mesh):
    fine = Mesh(mesh.devices.reshape(NX, NY, NZ4, NZ2, 2), ("x", "y", "z4", "z2", "depth"))
    return jax.shard_map(
        per_device,
        mesh=fine,
        in_specs=(P(ROW, "depth"), P("depth", ROW + Z), P(ROW)),
        out_specs=(P(ROW + ("depth",)), P(ROW, "depth")),
        check_vma=False,
    )
```
